32 devices in a mesh: row: 2 (over y), col: 4 (over x, core), rep: 4 (over z).
Axes of the slice: x: 2, y: 2, z: 4, core: 2. Of those that a mesh axis runs over, the one named last changes fastest.
Arguments:
- vectors: bfloat16 [2, 4, 8192, 128], P('row', 'col', 'rep'), may hold values from -6 to 6
- best_node: int32 [2, 4, 8192], P('row', 'col', 'rep'), may hold values from 0 to 16383, as said below
- codebook: bfloat16 [128, 1024, 128], P('row', ('col', 'rep')), may hold values from -6 to 6
Outputs:
- new_codebook: bfloat16 [128, 1024, 128], P('row', ('col', 'rep'))
The draws below stay inside these ranges and needn't reach their ends.
Inputs may be any that keep to these rules, and one draw needn't show every extreme that they name: Every entry of best_node is r * 256 + c for a node at row r and column c of its own node block.
All inputs are finite; a program needn't handle non-finite values.
Results may differ from the reference program's by a relative error of at most 0.0055.
Values may be sent and summed in bfloat16 or wider, within the bound.
No kernel may reach another device: no remote copies, remote signals or barrier semaphores. Data moves between devices by JAX's collectives and lax.ppermute only.
A program may use at most 64 MiB of HBM per device.

```python
import jax
import jax.numpy as jnp
from jax import lax

D = 128
BR = 64
BC = 256
RADIUS = 15
VEC_DEV = 2048
MR = 128
MC = 1024
N_ROW = 2
N_COL = 4
N_REP = 4


def node_index(key):
    total = VEC_DEV * N_REP
    shape = (N_ROW, N_COL, total)
    key_row, key_col = jax.random.split(jax.random.fold_in(key, 11))
    local_row = jax.random.randint(key_row, shape, 0, BR)
    local_col = jax.random.randint(key_col, shape, 0, BC)
    index = local_row * BC + local_col
    index = index.at[0, 0, 0].set(0)
    index = index.at[N_ROW - 1, N_COL - 1, total - 1].set(BR * BC - 1)
    return index.astype(jnp.int32)


def draw_best_node(key, part):
    return node_index(key)


def draw_vectors(key, part):
    index = node_index(key)
    shape = index.shape
    block_row = lax.broadcasted_iota(jnp.int32, shape, 0)
    block_col = lax.broadcasted_iota(jnp.int32, shape, 1)
    grid_row = (block_row * BR + index // BC).astype(jnp.float32)[..., None]
    grid_col = (block_col * BC + index % BC).astype(jnp.float32)[..., None]
    keys = jax.random.split(jax.random.fold_in(key, 23), 6)
    low = jnp.log(1.0 / 256.0)
    high = jnp.log(1.0 / 64.0)
    freq_row = jnp.exp(jax.random.uniform(keys[0], (D,), jnp.float32, low, high))
    freq_row = freq_row * jnp.where(jax.random.bernoulli(keys[1], 0.5, (D,)), 1.0, -1.0)
    freq_col = jnp.exp(jax.random.uniform(keys[2], (D,), jnp.float32, low, high))
    freq_col = freq_col * jnp.where(jax.random.bernoulli(keys[3], 0.5, (D,)), 1.0, -1.0)
    phase = jax.random.uniform(keys[4], (D,), jnp.float32, 0.0, 2.0 * jnp.pi)
    noise_key = jax.random.fold_in(key, 29)
    full_shape = shape + (D,)
    amp = jnp.exp(jax.random.uniform(keys[5], (D,), jnp.float32, jnp.log(0.6), jnp.log(2.0)))
    noise = jax.random.normal(noise_key, full_shape, jnp.float32)
    angle = 2.0 * jnp.pi * (grid_row * freq_row + grid_col * freq_col) + phase
    values = amp * jnp.sin(angle) + noise
    return jnp.clip(values, -6.0, 6.0).astype(jnp.bfloat16)


def levels(own_key, extent, cuts, smallest, top_value):
    def one(dim, parts):
        draws = jax.random.uniform(jax.random.fold_in(jax.random.fold_in(own_key, 6), dim), (parts,), jnp.float32, smallest / len(cuts), top_value / len(cuts))
        return jnp.repeat(jnp.exp(draws), extent[dim] // parts).reshape((-1,) + (1,) * (len(extent) - dim - 1))

    factor_of = one(*cuts[0])
    for cut in cuts[1:]:
        factor_of = factor_of * one(*cut)
    return factor_of


def normal_values(key, dims, width, bound, pieces=(), kind=jnp.bfloat16):
    array = width * jax.random.normal(key, dims, jnp.float32)
    if pieces:
        array = array * levels(key, dims, pieces, -0.22, 0.18)
    return jnp.clip(array, -bound, bound).astype(kind)


def setup_inputs(seed: int = 0) -> dict:
    key_list = jax.random.split(jax.random.key(seed), 4)
    vectors = draw_vectors(jax.random.fold_in(key_list[3], 71), 0)
    best_node = draw_best_node(jax.random.fold_in(key_list[3], 71), 0)
    codebook = normal_values(key_list[2], (MR, MC, D), 1.0, 6.0, ((0, 2), (1, 16)))
    return dict(vectors=vectors, best_node=best_node, codebook=codebook)


def kernel_taps():
    offsets = jnp.arange(-RADIUS, RADIUS + 1).astype(jnp.float32)
    return jnp.exp(-(offsets * offsets) / (2.0 * RADIUS * RADIUS))


def smooth_along(field, axis):
    taps = kernel_taps()
    length = field.shape[axis]
    widths = [(0, 0)] * field.ndim
    widths[axis] = (RADIUS, RADIUS)
    padded = jnp.pad(field, widths)
    total = jnp.zeros(field.shape, field.dtype)
    for step in range(2 * RADIUS + 1):
        total = total + taps[step] * lax.slice_in_dim(padded, step, step + length, axis=axis)
    return total


def reference(vectors, best_node, codebook):
    shape = best_node.shape
    block_row = lax.broadcasted_iota(jnp.int32, shape, 0)
    block_col = lax.broadcasted_iota(jnp.int32, shape, 1)
    local = best_node.astype(jnp.int32)
    global_idx = (block_row * BR + local // BC) * MC + block_col * BC + local % BC
    flat_vec = vectors.reshape(-1, D).astype(jnp.float32)
    flat_idx = global_idx.reshape(-1).astype(jnp.int32)
    numer = jax.ops.segment_sum(flat_vec, flat_idx, num_segments=MR * MC).reshape(MR, MC, D)
    ones = jnp.ones(flat_idx.shape, jnp.float32)
    counts = jax.ops.segment_sum(ones, flat_idx, num_segments=MR * MC).reshape(MR, MC)
    numer = smooth_along(smooth_along(numer, 0), 1)
    counts = smooth_along(smooth_along(counts, 0), 1)
    mean = numer / (counts[:, :, None] + 1.0)
    return (0.3 * codebook.astype(jnp.float32) + 0.7 * mean).astype(jnp.bfloat16)
```

```python
import functools
import math

import jax
import jax.numpy as jnp
from jax import lax
from jax.experimental import pallas as pl
from jax.experimental.pallas import tpu as pltpu
from jax.sharding import PartitionSpec as P

RADIUS = 15
LANES = 128
META = 16
HALO = 16
VMEM_LIMIT = 48 * 1024 * 1024


def gauss(distance):
    d = distance.astype(jnp.float32)
    weight = jnp.exp(-(d * d) / (2.0 * RADIUS * RADIUS))
    return jnp.where(jnp.abs(d) <= RADIUS, weight, 0.0)


def capacity(total, share):
    mean = total * share
    spread = math.sqrt(total * share * (1.0 - share))
    return min(-(-int(mean + 4.7 * spread) // 16) * 16, -(-total // 16) * 16)


def lane_rows(total):
    return -(-total // LANES)


def bucket_kernel(dims, edge, cap, scal_ref, x_ref, idx_ref, *rest):
    rows, block_cols, cols, reps = dims
    outs, onehot, table = rest[:reps], rest[reps], rest[reps + 1]
    me, turn, shift, low, high = (scal_ref[i] for i in range(5))
    idx = idx_ref[...]
    chunks = idx.shape[0]
    r = lax.div(idx, block_cols)
    c = idx - r * block_cols
    t = lax.div(c, cols)
    cl = c - t * cols
    step = partner_step(me, t, reps)
    member = [(step == s) for s in range(reps)]
    if edge:
        near = (r >= low) & (r < high)
        member = [m & near for m in member]
    members = jnp.concatenate([jnp.where(m, 1.0, 0.0) for m in member], axis=0)
    members16 = members.astype(jnp.bfloat16)
    count = reps * chunks
    up = lax.broadcasted_iota(jnp.int32, (LANES, LANES), 0)
    across = lax.broadcasted_iota(jnp.int32, (LANES, LANES), 1)
    tri = jnp.where(up <= across, 1.0, 0.0).astype(jnp.bfloat16)
    inside = jnp.dot(members16, tri, preferred_element_type=jnp.float32)
    ones = jnp.ones((LANES, LANES), jnp.bfloat16)
    totals = jnp.dot(members16, ones, preferred_element_type=jnp.float32)
    i0 = lax.broadcasted_iota(jnp.int32, (count, count), 0)
    i1 = lax.broadcasted_iota(jnp.int32, (count, count), 1)
    before = (lax.div(i0, chunks) == lax.div(i1, chunks)) & (i1 < i0)
    before = jnp.where(before, 1.0, 0.0).astype(jnp.bfloat16)
    offset = jnp.dot(before, totals.astype(jnp.bfloat16), preferred_element_type=jnp.float32)
    most = jnp.max(inside + offset)
    rounds = jnp.floor((most + (cap - 1)) / cap)
    place = inside + offset - 1.0 - (turn * cap).astype(jnp.float32)
    place = jnp.where(members > 0.5, place, -1.0).astype(jnp.int32)

    pad = jnp.zeros((LANES - 2 * chunks, LANES), jnp.float32)
    flat = jnp.concatenate([(r + shift).astype(jnp.float32), (cl + 1).astype(jnp.float32), pad], axis=0)
    table[...] = flat.T
    turned = table[...]
    extra = [
        (turned if k == 0 else pltpu.roll(turned, LANES - k, 1)).astype(jnp.bfloat16)
        for k in range(chunks)
    ]
    wide = jnp.concatenate([x_ref[...], jnp.concatenate(extra, axis=0)], axis=1)

    slot = lax.broadcasted_iota(jnp.int32, (cap, LANES), 0)
    pick_row = lax.broadcasted_iota(jnp.int32, (16, LANES), 0)
    pick_lane = lax.broadcasted_iota(jnp.int32, (16, LANES), 1)
    pick = ((pick_row == 0) & (pick_lane == 0)) | ((pick_row == 1) & (pick_lane == chunks))
    pick = jnp.where(pick, 1.0, 0.0).astype(jnp.bfloat16)
    for s in range(reps):
        for k in range(chunks):
            row = place[s * chunks + k : s * chunks + k + 1, :]
            onehot[:, k * LANES : (k + 1) * LANES] = jnp.where(slot == row, 1.0, 0.0).astype(jnp.bfloat16)
        moved = jnp.dot(onehot[...], wide, preferred_element_type=jnp.float32).astype(jnp.bfloat16)
        outs[s][:cap, :] = moved[:, :LANES]
        meta = lax.dot_general(
            pick, moved[:, LANES:], (((1,), (1,)), ((), ())), preferred_element_type=jnp.float32
        )
        outs[s][cap:, :] = meta_rows(meta[0:1], meta[1:2], rounds, cap).astype(jnp.bfloat16)


def meta_rows(node_row, node_col, rounds, cap):
    def split(line):
        parts = []
        for i in range(lane_rows(cap)):
            part = line[:, i * LANES : min((i + 1) * LANES, cap)]
            if part.shape[1] < LANES:
                part = jnp.concatenate([part, jnp.zeros((1, LANES - part.shape[1]), part.dtype)], axis=1)
            parts.append(part)
        return parts

    lines = split(node_col) + split(node_row) + [jnp.full((1, LANES), rounds, jnp.float32)]
    lines.append(jnp.zeros((META - len(lines), LANES), jnp.float32))
    return jnp.concatenate(lines, axis=0)


def partner_step(me, target, count):
    if count & (count - 1) == 0:
        return lax.bitwise_xor(target, jnp.full(target.shape, me, jnp.int32))
    return lax.rem(target - me + count, count)


def partner(me, step, count):
    return me ^ step if count & (count - 1) == 0 else (me + step) % count


def buckets(vec_rows, index_rows, scal, dims, edge, cap):
    reps = dims[3]
    total = vec_rows.shape[0]
    return pl.pallas_call(
        functools.partial(bucket_kernel, dims, edge, cap),
        out_shape=[jax.ShapeDtypeStruct((cap + META, LANES), jnp.bfloat16)] * reps,
        in_specs=[
            pl.BlockSpec(memory_space=pltpu.SMEM),
            pl.BlockSpec(memory_space=pltpu.VMEM),
            pl.BlockSpec(memory_space=pltpu.VMEM),
        ],
        out_specs=[pl.BlockSpec(memory_space=pltpu.VMEM)] * reps,
        scratch_shapes=[
            pltpu.VMEM((cap, total), jnp.bfloat16),
            pltpu.VMEM((LANES, LANES), jnp.float32),
        ],
        compiler_params=pltpu.CompilerParams(vmem_limit_bytes=VMEM_LIMIT),
        cost_estimate=pl.CostEstimate(
            flops=2 * reps * cap * total * 256, bytes_accessed=2 * total * LANES * 2, transcendentals=0
        ),
        name="buckets",
    )(scal, vec_rows, index_rows)


GROUP = 16


def sums_kernel(dims, caps, first, last, *refs):
    rows, cols = dims
    refs = list(refs)
    messages = [refs.pop(0) for _ in caps]
    if not first:
        flag_in, acc_in, cnt_in = refs.pop(0), refs.pop(0), refs.pop(0)
    flag, acc, cnt = refs.pop(0), refs.pop(0), refs.pop(0)
    if last:
        own, left, right = refs.pop(0), refs.pop(0), refs.pop(0)
    weights, columns, product = refs[: len(caps)], refs[len(caps) : 2 * len(caps)], refs[2 * len(caps) :]
    step = pl.program_id(0)

    @pl.when(step == 0)
    def _():
        counted = jnp.zeros((cols, rows), jnp.float32) if first else cnt_in[...]
        rounds = jnp.float32(0.0)
        for m, message in enumerate(messages):
            cap = caps[m]
            lines = lane_rows(cap)
            meta = message[cap:, :].astype(jnp.float32)
            width = cap + META
            line = lambda i: jnp.concatenate([meta[i + j : i + j + 1] for j in range(lines)], axis=1)
            node_col, node_row = line(0)[:, :width], line(lines)[:, :width]
            if node_col.shape[1] < width:
                fill = jnp.zeros((1, width - node_col.shape[1]), jnp.float32)
                node_col = jnp.concatenate([node_col, fill], axis=1)
                node_row = jnp.concatenate([node_row, fill], axis=1)
            rounds = jnp.maximum(rounds, jnp.max(meta[2 * lines : 2 * lines + 1]))
            here = lax.broadcasted_iota(jnp.int32, (cols, width), 0).astype(jnp.float32)
            hit = jnp.where(here == node_col - 1.0, 1.0, 0.0).astype(jnp.bfloat16)
            columns[m][...] = hit
            at = lax.broadcasted_iota(jnp.int32, (rows, width), 0).astype(jnp.float32)
            weight = gauss(at - node_row).astype(jnp.bfloat16)
            weights[m][...] = weight.astype(jnp.float32)
            counted = counted + lax.dot_general(
                hit, weight, (((1,), (1,)), ((), ())), preferred_element_type=jnp.float32
            )
        cnt[...] = counted
        rounds = rounds.astype(jnp.int32)
        flag[0] = rounds if first else jnp.maximum(rounds, flag_in[0])
        if last:
            fill = jnp.zeros((cols, LANES - rows), jnp.float32) if rows < LANES else None
            lane_counts = counted if fill is None else jnp.concatenate([counted, fill], axis=1)
            lane_counts = lane_counts.astype(jnp.bfloat16)
            left[rows : rows + 1] = lane_counts[:HALO][None]
            right[rows : rows + 1] = lane_counts[cols - HALO :][None]

    start = pl.multiple_of(step * GROUP, GROUP)
    total = jnp.zeros((GROUP * cols, LANES), jnp.float32)
    for m, message in enumerate(messages):
        width = caps[m] + META
        hit = columns[m][...]
        block = weights[m][pl.ds(start, GROUP), :]
        for i in range(GROUP):
            line = jnp.broadcast_to(block[i : i + 1, :], (cols, width)).astype(jnp.bfloat16)
            product[m][i * cols : (i + 1) * cols, :] = hit * line
        total = total + jnp.dot(product[m][...], message[...], preferred_element_type=jnp.float32)
    total = total.reshape(GROUP, cols, LANES)
    if not first:
        total = total + acc_in[...]
    acc[...] = total
    if last:
        rounded = total.astype(jnp.bfloat16)
        own[...] = rounded
        left[pl.ds(start, GROUP)] = rounded[:, :HALO, :]
        right[pl.ds(start, GROUP)] = rounded[:, cols - HALO :, :]


def sums(messages, state, last, dims):
    rows, cols = dims
    caps = [m.shape[0] - META for m in messages]
    first = state is None
    smem = pl.BlockSpec(memory_space=pltpu.SMEM)
    whole = pl.BlockSpec(memory_space=pltpu.VMEM)
    part = pl.BlockSpec((GROUP, cols, LANES), lambda i: (i, 0, 0))
    acc_shape = [
        jax.ShapeDtypeStruct((1,), jnp.int32),
        jax.ShapeDtypeStruct((rows, cols, LANES), jnp.float32),
        jax.ShapeDtypeStruct((cols, rows), jnp.float32),
    ]
    out_shape, out_specs = list(acc_shape), [smem, part, whole]
    if last:
        halo = jax.ShapeDtypeStruct((rows + 1, HALO, LANES), jnp.bfloat16)
        out_shape += [jax.ShapeDtypeStruct((rows, cols, LANES), jnp.bfloat16), halo, halo]
        out_specs += [part, whole, whole]
    in_specs = [whole] * len(messages)
    operands = list(messages)
    if not first:
        in_specs += [smem, part, whole]
        operands += list(state[:3])
    scratch = [pltpu.VMEM((rows, c + META), jnp.float32) for c in caps]
    scratch += [pltpu.VMEM((cols, c + META), jnp.bfloat16) for c in caps]
    scratch += [pltpu.VMEM((GROUP * cols, c + META), jnp.bfloat16) for c in caps]
    deep = sum(c + META for c in caps)
    return pl.pallas_call(
        functools.partial(sums_kernel, dims, caps, first, last),
        grid=(rows // GROUP,),
        out_shape=out_shape,
        in_specs=in_specs,
        out_specs=out_specs,
        scratch_shapes=scratch,
        compiler_params=pltpu.CompilerParams(vmem_limit_bytes=VMEM_LIMIT),
        cost_estimate=pl.CostEstimate(
            flops=2 * rows * cols * deep * 256, bytes_accessed=8 * rows * cols * LANES, transcendentals=0
        ),
        name="sums",
    )(*operands)


def mix_kernel(dims, own, left, right, cnt, codebook, out, scale, band):
    rows, cols = dims
    step = pl.program_id(0)
    deep = cols + 2 * HALO

    @pl.when(step == 0)
    def _():
        to = lax.broadcasted_iota(jnp.int32, (cols, deep), 0)
        frm = lax.broadcasted_iota(jnp.int32, (cols, deep), 1) - HALO
        weight = gauss(frm - to).astype(jnp.bfloat16)
        band[...] = weight
        near = lambda ref: ref[rows].astype(jnp.float32)[:, :rows]
        counted = jnp.concatenate([near(left), cnt[...], near(right)], axis=0).astype(jnp.bfloat16)
        smooth = jnp.dot(weight, counted, preferred_element_type=jnp.float32)
        scale[...] = 0.7 / (smooth + 1.0)

    for i in range(GROUP):
        a = step * GROUP + i
        deep_rows = jnp.concatenate([left[a], own[i], right[a]], axis=0)
        smooth = jnp.dot(band[...], deep_rows, preferred_element_type=jnp.float32)
        lane = lax.broadcasted_iota(jnp.int32, (cols, rows), 1)
        factor = jnp.sum(jnp.where(lane == a, scale[...], 0.0), axis=1, keepdims=True)
        out[i] = (0.3 * codebook[i].astype(jnp.float32) + smooth * factor).astype(jnp.bfloat16)


def mix(own, left, right, cnt, codebook):
    rows, cols, width = codebook.shape
    part = pl.BlockSpec((GROUP, cols, width), lambda i: (i, 0, 0))
    whole = pl.BlockSpec(memory_space=pltpu.VMEM)
    return pl.pallas_call(
        functools.partial(mix_kernel, (rows, cols)),
        grid=(rows // GROUP,),
        out_shape=jax.ShapeDtypeStruct(codebook.shape, jnp.bfloat16),
        in_specs=[part, whole, whole, whole, part],
        out_specs=part,
        scratch_shapes=[
            pltpu.VMEM((cols, rows), jnp.float32),
            pltpu.VMEM((cols, cols + 2 * HALO), jnp.bfloat16),
        ],
        compiler_params=pltpu.CompilerParams(vmem_limit_bytes=VMEM_LIMIT),
        name="mix",
    )(own, left, right, cnt, codebook)


def body(vectors, best_node, codebook):
    rows, cols, width = codebook.shape
    reps, bands = lax.axis_size("rep"), lax.axis_size("row")
    dims = (rows, cols * reps, cols, reps)
    vec_rows = vectors.reshape(-1, width)
    total = vec_rows.shape[0]
    index_rows = best_node.reshape(-1, LANES)
    me, band = lax.axis_index("rep"), lax.axis_index("row")
    cap = capacity(total, 1.0 / reps)
    edge_cap = capacity(total, RADIUS / rows / reps)
    zero = jnp.int32(0)

    if bands == 2:
        shift = jnp.where(band == 0, -rows, rows)
        low = jnp.where(band == 0, rows - RADIUS, 0)
        sides = [([(0, 1), (1, 0)], shift, low, low + RADIUS)]
    else:
        sides = [
            ([(i, i + 1) for i in range(bands - 1)], -rows, rows - RADIUS, rows),
            ([(i + 1, i) for i in range(bands - 1)], rows, 0, RADIUS),
        ]

    def one_round(turn):
        mine = buckets(vec_rows, index_rows, jnp.stack([me, turn, zero, zero, zero]), dims, False, cap)
        arrived = [
            lax.ppermute(mine[s], "rep", [(i, partner(i, s, reps)) for i in range(reps)])
            for s in range(1, reps)
        ]
        edges = []
        for pairs, shift, low, high in sides:
            scal = jnp.stack([me, turn, jnp.int32(shift), jnp.int32(low), jnp.int32(high)])
            for s, message in enumerate(buckets(vec_rows, index_rows, scal, dims, True, edge_cap)):
                joint = [(a * reps + i, b * reps + partner(i, s, reps)) for a, b in pairs for i in range(reps)]
                edges.append(lax.ppermute(message, ("row", "rep"), joint))
        return mine[0], edges, arrived

    def add_all(state, turn):
        own, edges, arrived = one_round(turn)
        state = sums([own], state, False, (rows, cols))
        if edges:
            state = sums(edges, state, False, (rows, cols))
        for n, message in enumerate(arrived):
            state = sums([message], state, n == len(arrived) - 1, (rows, cols))
        flag, acc, cnt, here, left, right = state
        if bands != 2:
            flag = lax.pmax(flag, ("row", "rep"))
        return flag, acc, cnt, here, left, right

    state = add_all(None, zero)

    def more(carry):
        return carry[0] < carry[1][0]

    def again(carry):
        turn, *state = carry
        return (turn + 1, *add_all(state, turn))

    _, _, _, cnt, here, left, right = lax.while_loop(more, again, (jnp.int32(1), *state))
    peers = lax.axis_size(("col", "rep"))
    from_left = lax.ppermute(right, ("col", "rep"), [(i, i + 1) for i in range(peers - 1)])
    from_right = lax.ppermute(left, ("col", "rep"), [(i + 1, i) for i in range(peers - 1)])
    return mix(here, from_left, from_right, cnt, codebook)


def solution(mesh):
    placed = (P("row", "col", "rep", None), P("row", "col", "rep"), P("row", ("col", "rep"), None))
    return jax.shard_map(
        body, mesh=mesh, in_specs=placed, out_specs=P("row", ("col", "rep"), None), check_vma=False
    )
```

```python
import functools
import math

import jax
import jax.numpy as jnp
from jax import lax
from jax.experimental import pallas as pl
from jax.experimental.pallas import tpu as pltpu
from jax.sharding import PartitionSpec as P

RADIUS = 15
LANES = 128
META = 16
HALO = 16
VMEM_LIMIT = 48 * 1024 * 1024


def gauss(distance):
    d = distance.astype(jnp.float32)
    weight = jnp.exp(-(d * d) / (2.0 * RADIUS * RADIUS))
    return jnp.where(jnp.abs(d) <= RADIUS, weight, 0.0)


def capacity(total, share):
    mean = total * share
    spread = math.sqrt(total * share * (1.0 - share))
    return min(-(-int(mean + 4.7 * spread) // 16) * 16, -(-total // 16) * 16)


def quotient(value, by):
    if by & (by - 1) == 0:
        return lax.shift_right_logical(value, by.bit_length() - 1)
    return lax.div(value, by)


def lane_rows(total):
    return -(-total // LANES)


CHUNK = 256
WINDOWS = (48, 96)


def bucket_kernel(dims, caps, scal_ref, x_ref, idx_ref, *rest):
    rows, block_cols, cols, reps = dims
    cap, edge_cap = caps
    owns, edges = rest[:reps], rest[reps : 2 * reps]
    wide, moved, edge_moved, onehot = rest[2 * reps :]
    me, turn, shift, low, high = (scal_ref[i] for i in range(5))
    idx = idx_ref[...]
    chunks = idx.shape[0]
    r = quotient(idx, block_cols)
    c = idx - r * block_cols
    t = quotient(c, cols)
    cl = c - t * cols
    step = partner_step(me, t, reps)
    near = (r >= low) & (r < high)
    member = []
    for s in range(reps):
        here = step == s
        member += [here & near, here & jnp.logical_not(near)]
    members = jnp.concatenate([jnp.where(m, 1.0, 0.0) for m in member], axis=0)
    members16 = members.astype(jnp.bfloat16)
    count = 2 * reps * chunks
    up = lax.broadcasted_iota(jnp.int32, (LANES, LANES), 0)
    across = lax.broadcasted_iota(jnp.int32, (LANES, LANES), 1)
    tri = jnp.where(up <= across, 1.0, 0.0).astype(jnp.bfloat16)
    ones = jnp.ones((LANES, LANES), jnp.bfloat16)
    both = jnp.concatenate([tri, ones], axis=1)
    scanned = jnp.dot(members16, both, preferred_element_type=jnp.float32)
    inside, totals = scanned[:, :LANES], scanned[:, LANES:]
    i0 = lax.broadcasted_iota(jnp.int32, (count, count), 0)
    i1 = lax.broadcasted_iota(jnp.int32, (count, count), 1)
    group = 2 * chunks
    before = (quotient(i0, group) == quotient(i1, group)) & (i1 < i0)
    before = jnp.where(before, 1.0, 0.0).astype(jnp.bfloat16)
    offset = jnp.dot(before, totals.astype(jnp.bfloat16), preferred_element_type=jnp.float32)
    place = jnp.where(members > 0.5, offset + inside - 1.0, -1.0)
    ends = offset + totals
    near_count = [ends[s * group + chunks - 1 : s * group + chunks] for s in range(reps)]
    own_count = [ends[(s + 1) * group - 1 : (s + 1) * group] for s in range(reps)]
    most = functools.reduce(jnp.maximum, own_count)
    most_near = functools.reduce(jnp.maximum, near_count)
    rounds = jnp.maximum(
        jnp.floor((most + (cap - 0.5)) / cap), jnp.floor((most_near + (edge_cap - 0.5)) / edge_cap)
    )

    pad = jnp.zeros((LANES - 2 * chunks, LANES), jnp.float32)
    flat = jnp.concatenate([r.astype(jnp.float32), (cl + 1).astype(jnp.float32), pad], axis=0)
    turned = flat.T
    wide[:, :LANES] = x_ref[...]
    for k in range(chunks):
        part = turned if k == 0 else pltpu.roll(turned, LANES - k, 1)
        wide[k * LANES : (k + 1) * LANES, LANES:] = part.astype(jnp.bfloat16)

    per = CHUNK // LANES
    begin = jnp.floor(offset / 8.0) * 8.0
    fits = turn == 0
    spill = jnp.float32(0.0)
    for e, window in enumerate(WINDOWS):
        for s in range(reps):
            lines = slice((2 * s + e) * chunks, (2 * s + e + 1) * chunks)
            worst = ends[lines]
            first_line = begin[lines]
            for j in range(chunks // per):
                room = worst[(j + 1) * per - 1 : (j + 1) * per] - first_line[j * per : j * per + 1]
                spill = jnp.maximum(spill, room - window)
    fits = fits & (jnp.max(spill) <= 0.0) & (jnp.max(most) <= cap)

    @pl.when(fits)
    def _():
        moved[...] = jnp.zeros_like(moved)
        starts = begin.astype(jnp.int32)
        for j in range(chunks // per):
            pieces, spots = [], []
            for s in range(reps):
                for e, window in enumerate(WINDOWS):
                    line = (2 * s + e) * chunks + j * per
                    slot = lax.broadcasted_iota(jnp.int32, (window, LANES), 0).astype(jnp.float32)
                    halves = []
                    for h in range(per):
                        target = place[line + h : line + h + 1] - begin[line : line + 1]
                        halves.append(jnp.where(slot == target, 1.0, 0.0).astype(jnp.bfloat16))
                    pieces.append(jnp.concatenate(halves, axis=1))
                    spots.append((s, window, starts[line, 0]))
            picked = jnp.dot(
                jnp.concatenate(pieces, axis=0),
                wide[j * CHUNK : (j + 1) * CHUNK, :],
                preferred_element_type=jnp.float32,
            )
            at = 0
            for s, window, spot in spots:
                span = pl.ds(pl.multiple_of(spot, 8), window)
                moved[s, span, :] = moved[s, span, :] + picked[at : at + window]
                at += window
        for s in range(reps):
            edge_moved[s] = moved[s, :edge_cap, :]

    @pl.when(jnp.logical_not(fits))
    def _():
        def gather(s, lines, size, out):
            slot = lax.broadcasted_iota(jnp.int32, (size, LANES), 0).astype(jnp.float32)
            slot = slot + (turn * size).astype(jnp.float32)
            for k in range(chunks):
                part = jnp.zeros((size, LANES), jnp.float32)
                for line in lines:
                    row = place[line * chunks + k : line * chunks + k + 1]
                    part = part + jnp.where(slot == row, 1.0, 0.0)
                onehot[:size, k * LANES : (k + 1) * LANES] = part.astype(jnp.bfloat16)
            out[s, :size, :] = jnp.dot(onehot[:size, :], wide[...], preferred_element_type=jnp.float32)

        for s in range(reps):
            gather(s, (2 * s, 2 * s + 1), cap, moved)
            gather(s, (2 * s,), edge_cap, edge_moved)

    pick_row = lax.broadcasted_iota(jnp.int32, (16, LANES), 0)
    pick_lane = lax.broadcasted_iota(jnp.int32, (16, LANES), 1)
    pick = ((pick_row == 0) & (pick_lane == 0)) | ((pick_row == 1) & (pick_lane == chunks))
    pick = jnp.where(pick, 1.0, 0.0).astype(jnp.bfloat16)
    for s in range(reps):
        for size, source, out in ((cap, moved, owns[s]), (edge_cap, edge_moved, edges[s])):
            ready = source[s, :size, :].astype(jnp.bfloat16)
            out[:size, :] = ready[:, :LANES]
            meta = lax.dot_general(
                pick, ready[:, LANES:], (((1,), (1,)), ((), ())), preferred_element_type=jnp.float32
            )
            node_row, node_col = meta[0:1], meta[1:2]
            if out is edges[s]:
                number = lax.broadcasted_iota(jnp.int32, (1, size), 1) + turn * size
                listed = number.astype(jnp.float32) < near_count[s][:, :1]
                node_col = jnp.where(listed, node_col, 0.0)
                node_row = node_row + shift.astype(jnp.float32)
            out[size:, :] = meta_rows(node_row, node_col, rounds, size).astype(jnp.bfloat16)


def meta_rows(node_row, node_col, rounds, cap):
    def split(line):
        parts = []
        for i in range(lane_rows(cap)):
            part = line[:, i * LANES : min((i + 1) * LANES, cap)]
            if part.shape[1] < LANES:
                part = jnp.concatenate([part, jnp.zeros((1, LANES - part.shape[1]), part.dtype)], axis=1)
            parts.append(part)
        return parts

    lines = split(node_col) + split(node_row) + [rounds]
    lines.append(jnp.zeros((META - len(lines), LANES), jnp.float32))
    return jnp.concatenate(lines, axis=0)


def partner_step(me, target, count):
    if count & (count - 1) == 0:
        return lax.bitwise_xor(target, jnp.full(target.shape, me, jnp.int32))
    return lax.rem(target - me + count, count)


def partner(me, step, count):
    return me ^ step if count & (count - 1) == 0 else (me + step) % count


def buckets(vec_rows, index_rows, scal, dims, caps):
    reps = dims[3]
    total = vec_rows.shape[0]
    deep = max(caps) + max(WINDOWS)
    messages = [jax.ShapeDtypeStruct((c + META, LANES), jnp.bfloat16) for c in caps for _ in range(reps)]
    whole = pl.BlockSpec(memory_space=pltpu.VMEM)
    out = pl.pallas_call(
        functools.partial(bucket_kernel, dims, caps),
        out_shape=messages,
        in_specs=[pl.BlockSpec(memory_space=pltpu.SMEM), whole, whole],
        out_specs=[whole] * (2 * reps),
        scratch_shapes=[
            pltpu.VMEM((total, 2 * LANES), jnp.bfloat16),
            pltpu.VMEM((reps, deep, 2 * LANES), jnp.float32),
            pltpu.VMEM((reps, caps[1], 2 * LANES), jnp.float32),
            pltpu.VMEM((max(caps), total), jnp.bfloat16),
        ],
        compiler_params=pltpu.CompilerParams(vmem_limit_bytes=VMEM_LIMIT),
        cost_estimate=pl.CostEstimate(
            flops=2 * reps * 1024 * total * 256, bytes_accessed=2 * total * LANES * 2, transcendentals=0
        ),
        name="buckets",
    )(scal, vec_rows, index_rows)
    return out[:reps], out[reps:]


GROUP = 16


def sums_kernel(dims, caps, first, last, *refs):
    rows, cols = dims
    refs = list(refs)
    messages = [refs.pop(0) for _ in caps]
    if not first:
        flag_in, acc_in, cnt_in = refs.pop(0), refs.pop(0), refs.pop(0)
    flag, acc, cnt = refs.pop(0), refs.pop(0), refs.pop(0)
    if last:
        own, left, right = refs.pop(0), refs.pop(0), refs.pop(0)
    weights, columns, product = refs[: len(caps)], refs[len(caps) : 2 * len(caps)], refs[2 * len(caps) :]
    step = pl.program_id(0)

    @pl.when(step == 0)
    def _():
        counted = jnp.zeros((cols, rows), jnp.float32) if first else cnt_in[...]
        rounds = jnp.float32(0.0)
        for m, message in enumerate(messages):
            cap = caps[m]
            lines = lane_rows(cap)
            meta = message[cap:, :].astype(jnp.float32)
            width = cap + META
            line = lambda i: jnp.concatenate([meta[i + j : i + j + 1] for j in range(lines)], axis=1)
            node_col, node_row = line(0)[:, :width], line(lines)[:, :width]
            if node_col.shape[1] < width:
                fill = jnp.zeros((1, width - node_col.shape[1]), jnp.float32)
                node_col = jnp.concatenate([node_col, fill], axis=1)
                node_row = jnp.concatenate([node_row, fill], axis=1)
            rounds = jnp.maximum(rounds, jnp.max(meta[2 * lines : 2 * lines + 1]))
            here = lax.broadcasted_iota(jnp.int32, (cols, width), 0).astype(jnp.float32)
            hit = jnp.where(here == node_col - 1.0, 1.0, 0.0).astype(jnp.bfloat16)
            columns[m][...] = hit
            at = lax.broadcasted_iota(jnp.int32, (rows, width), 0).astype(jnp.float32)
            weight = gauss(at - node_row).astype(jnp.bfloat16)
            weights[m][...] = weight.astype(jnp.float32)
            counted = counted + lax.dot_general(
                hit, weight, (((1,), (1,)), ((), ())), preferred_element_type=jnp.float32
            )
        cnt[...] = counted
        rounds = rounds.astype(jnp.int32)
        flag[0] = rounds if first else jnp.maximum(rounds, flag_in[0])
        if last:
            fill = jnp.zeros((cols, LANES - rows), jnp.float32) if rows < LANES else None
            lane_counts = counted if fill is None else jnp.concatenate([counted, fill], axis=1)
            lane_counts = lane_counts.astype(jnp.bfloat16)
            left[rows : rows + 1] = lane_counts[:HALO][None]
            right[rows : rows + 1] = lane_counts[cols - HALO :][None]

    start = pl.multiple_of(step * GROUP, GROUP)
    total = jnp.zeros((GROUP * cols, LANES), jnp.float32)
    for m, message in enumerate(messages):
        width = caps[m] + META
        hit = columns[m][...]
        block = weights[m][pl.ds(start, GROUP), :]
        for i in range(GROUP):
            line = jnp.broadcast_to(block[i : i + 1, :], (cols, width)).astype(jnp.bfloat16)
            product[m][i * cols : (i + 1) * cols, :] = hit * line
        total = total + jnp.dot(product[m][...], message[...], preferred_element_type=jnp.float32)
    total = total.reshape(GROUP, cols, LANES)
    if not first:
        total = total + acc_in[...]
    acc[...] = total
    if last:
        rounded = total.astype(jnp.bfloat16)
        own[...] = rounded
        left[pl.ds(start, GROUP)] = rounded[:, :HALO, :]
        right[pl.ds(start, GROUP)] = rounded[:, cols - HALO :, :]


def sums(messages, state, last, dims):
    rows, cols = dims
    caps = [m.shape[0] - META for m in messages]
    first = state is None
    smem = pl.BlockSpec(memory_space=pltpu.SMEM)
    whole = pl.BlockSpec(memory_space=pltpu.VMEM)
    part = pl.BlockSpec((GROUP, cols, LANES), lambda i: (i, 0, 0))
    acc_shape = [
        jax.ShapeDtypeStruct((1,), jnp.int32),
        jax.ShapeDtypeStruct((rows, cols, LANES), jnp.float32),
        jax.ShapeDtypeStruct((cols, rows), jnp.float32),
    ]
    out_shape, out_specs = list(acc_shape), [smem, part, whole]
    if last:
        halo = jax.ShapeDtypeStruct((rows + 1, HALO, LANES), jnp.bfloat16)
        out_shape += [jax.ShapeDtypeStruct((rows, cols, LANES), jnp.bfloat16), halo, halo]
        out_specs += [part, whole, whole]
    in_specs = [whole] * len(messages)
    operands = list(messages)
    if not first:
        in_specs += [smem, part, whole]
        operands += list(state[:3])
    scratch = [pltpu.VMEM((rows, c + META), jnp.float32) for c in caps]
    scratch += [pltpu.VMEM((cols, c + META), jnp.bfloat16) for c in caps]
    scratch += [pltpu.VMEM((GROUP * cols, c + META), jnp.bfloat16) for c in caps]
    deep = sum(c + META for c in caps)
    return pl.pallas_call(
        functools.partial(sums_kernel, dims, caps, first, last),
        grid=(rows // GROUP,),
        out_shape=out_shape,
        in_specs=in_specs,
        out_specs=out_specs,
        scratch_shapes=scratch,
        compiler_params=pltpu.CompilerParams(vmem_limit_bytes=VMEM_LIMIT),
        cost_estimate=pl.CostEstimate(
            flops=2 * rows * cols * deep * 256, bytes_accessed=8 * rows * cols * LANES, transcendentals=0
        ),
        name="sums",
    )(*operands)


def mix_kernel(dims, own, left, right, cnt, codebook, out, scale, band):
    rows, cols = dims
    step = pl.program_id(0)
    deep = cols + 2 * HALO

    @pl.when(step == 0)
    def _():
        to = lax.broadcasted_iota(jnp.int32, (cols, deep), 0)
        frm = lax.broadcasted_iota(jnp.int32, (cols, deep), 1) - HALO
        weight = gauss(frm - to).astype(jnp.bfloat16)
        band[...] = weight
        near = lambda ref: ref[rows].astype(jnp.float32)[:, :rows]
        counted = jnp.concatenate([near(left), cnt[...], near(right)], axis=0).astype(jnp.bfloat16)
        smooth = jnp.dot(weight, counted, preferred_element_type=jnp.float32)
        scale[...] = 0.7 / (smooth + 1.0)

    for i in range(GROUP):
        a = step * GROUP + i
        deep_rows = jnp.concatenate([left[a], own[i], right[a]], axis=0)
        smooth = jnp.dot(band[...], deep_rows, preferred_element_type=jnp.float32)
        lane = lax.broadcasted_iota(jnp.int32, (cols, rows), 1)
        factor = jnp.sum(jnp.where(lane == a, scale[...], 0.0), axis=1, keepdims=True)
        out[i] = (0.3 * codebook[i].astype(jnp.float32) + smooth * factor).astype(jnp.bfloat16)


def mix(own, left, right, cnt, codebook):
    rows, cols, width = codebook.shape
    part = pl.BlockSpec((GROUP, cols, width), lambda i: (i, 0, 0))
    whole = pl.BlockSpec(memory_space=pltpu.VMEM)
    return pl.pallas_call(
        functools.partial(mix_kernel, (rows, cols)),
        grid=(rows // GROUP,),
        out_shape=jax.ShapeDtypeStruct(codebook.shape, jnp.bfloat16),
        in_specs=[part, whole, whole, whole, part],
        out_specs=part,
        scratch_shapes=[
            pltpu.VMEM((cols, rows), jnp.float32),
            pltpu.VMEM((cols, cols + 2 * HALO), jnp.bfloat16),
        ],
        compiler_params=pltpu.CompilerParams(vmem_limit_bytes=VMEM_LIMIT),
        name="mix",
    )(own, left, right, cnt, codebook)


def body(vectors, best_node, codebook):
    rows, cols, width = codebook.shape
    reps, bands = lax.axis_size("rep"), lax.axis_size("row")
    dims = (rows, cols * reps, cols, reps)
    vec_rows = vectors.reshape(-1, width)
    total = vec_rows.shape[0]
    index_rows = best_node.reshape(-1, LANES)
    me, band = lax.axis_index("rep"), lax.axis_index("row")
    cap = capacity(total, 1.0 / reps)
    edge_cap = capacity(total, RADIUS / rows / reps)
    zero = jnp.int32(0)

    if bands == 2:
        shift = jnp.where(band == 0, -rows, rows)
        low = jnp.where(band == 0, rows - RADIUS, 0)
        sides = [([(0, 1), (1, 0)], shift, low, low + RADIUS)]
    else:
        sides = [
            ([(i, i + 1) for i in range(bands - 1)], -rows, rows - RADIUS, rows),
            ([(i + 1, i) for i in range(bands - 1)], rows, 0, RADIUS),
        ]

    def one_round(turn):
        mine, arrived, edges = None, [], []
        for pairs, shift, low, high in sides:
            scal = jnp.stack([me, turn, jnp.int32(shift), jnp.int32(low), jnp.int32(high)])
            own, near = buckets(vec_rows, index_rows, scal, dims, (cap, edge_cap))
            if mine is None:
                mine = own[0]
                arrived = [
                    lax.ppermute(own[s], "rep", [(i, partner(i, s, reps)) for i in range(reps)])
                    for s in range(1, reps)
                ]
            for s, message in enumerate(near):
                joint = [(a * reps + i, b * reps + partner(i, s, reps)) for a, b in pairs for i in range(reps)]
                edges.append(lax.ppermute(message, ("row", "rep"), joint))
        return mine, edges, arrived

    def add_all(state, turn):
        own, edges, arrived = one_round(turn)
        state = sums([own], state, False, (rows, cols))
        state = sums(edges, state, False, (rows, cols))
        for n, message in enumerate(arrived):
            state = sums([message], state, n == len(arrived) - 1, (rows, cols))
        flag, acc, cnt, here, left, right = state
        if bands != 2:
            flag = lax.pmax(flag, ("row", "rep"))
        return flag, acc, cnt, here, left, right

    state = add_all(None, zero)

    def more(carry):
        return carry[0] < carry[1][0]

    def again(carry):
        turn, *state = carry
        return (turn + 1, *add_all(state, turn))

    _, _, _, cnt, here, left, right = lax.while_loop(more, again, (jnp.int32(1), *state))
    peers = lax.axis_size(("col", "rep"))
    from_left = lax.ppermute(right, ("col", "rep"), [(i, i + 1) for i in range(peers - 1)])
    from_right = lax.ppermute(left, ("col", "rep"), [(i + 1, i) for i in range(peers - 1)])
    return mix(here, from_left, from_right, cnt, codebook)


def solution(mesh):
    placed = (P("row", "col", "rep", None), P("row", "col", "rep"), P("row", ("col", "rep"), None))
    return jax.shard_map(
        body, mesh=mesh, in_specs=placed, out_specs=P("row", ("col", "rep"), None), check_vma=False
    )
```

```python
import functools
import math

import jax
import jax.numpy as jnp
from jax import lax
from jax.experimental import pallas as pl
from jax.experimental.pallas import tpu as pltpu
from jax.sharding import PartitionSpec as P

RADIUS = 15
LANES = 128
META = 16
HALO = 16
VMEM_LIMIT = 24 * 1024 * 1024
ORDER = True
COST = pl.CostEstimate(flops=2**20, bytes_accessed=2**16, transcendentals=0)


def gauss(distance):
    d = distance.astype(jnp.float32)
    weight = jnp.exp(-(d * d) / (2.0 * RADIUS * RADIUS))
    return jnp.where(jnp.abs(d) <= RADIUS, weight, 0.0)


def capacity(total, share):
    mean = total * share
    spread = math.sqrt(total * share * (1.0 - share))
    return min(-(-int(mean + 4.7 * spread) // 16) * 16, -(-total // 16) * 16)


def quotient(value, by):
    if by & (by - 1) == 0:
        return lax.shift_right_logical(value, by.bit_length() - 1)
    return lax.div(value, by)


def lane_rows(total):
    return -(-total // LANES)


CHUNK = 256
WINDOWS = (48, 96)


def bucket_kernel(dims, caps, scal_ref, x_ref, idx_ref, *rest):
    rows, block_cols, cols, reps = dims
    cap, edge_cap = caps
    owns, edges = rest[:reps], rest[reps : 2 * reps]
    wide, moved, edge_moved, onehot = rest[2 * reps :]
    me, turn, shift, low, high = (scal_ref[i] for i in range(5))
    idx = idx_ref[...]
    chunks = idx.shape[0]
    r = quotient(idx, block_cols)
    c = idx - r * block_cols
    t = quotient(c, cols)
    cl = c - t * cols
    step = partner_step(me, t, reps)
    near = (r >= low) & (r < high)
    member = []
    for s in range(reps):
        here = step == s
        member += [here & near, here & jnp.logical_not(near)]
    members = jnp.concatenate([jnp.where(m, 1.0, 0.0) for m in member], axis=0)
    members16 = members.astype(jnp.bfloat16)
    count = 2 * reps * chunks
    up = lax.broadcasted_iota(jnp.int32, (LANES, LANES), 0)
    across = lax.broadcasted_iota(jnp.int32, (LANES, LANES), 1)
    tri = jnp.where(up <= across, 1.0, 0.0).astype(jnp.bfloat16)
    ones = jnp.ones((LANES, LANES), jnp.bfloat16)
    both = jnp.concatenate([tri, ones], axis=1)
    scanned = jnp.dot(members16, both, preferred_element_type=jnp.float32)
    inside, totals = scanned[:, :LANES], scanned[:, LANES:]
    i0 = lax.broadcasted_iota(jnp.int32, (count, count), 0)
    i1 = lax.broadcasted_iota(jnp.int32, (count, count), 1)
    group = 2 * chunks
    before = (quotient(i0, group) == quotient(i1, group)) & (i1 < i0)
    before = jnp.where(before, 1.0, 0.0).astype(jnp.bfloat16)
    offset = jnp.dot(before, totals.astype(jnp.bfloat16), preferred_element_type=jnp.float32)
    place = jnp.where(members > 0.5, offset + inside - 1.0, -1.0)
    ends = offset + totals
    near_count = [ends[s * group + chunks - 1 : s * group + chunks] for s in range(reps)]
    own_count = [ends[(s + 1) * group - 1 : (s + 1) * group] for s in range(reps)]
    most = functools.reduce(jnp.maximum, own_count)
    most_near = functools.reduce(jnp.maximum, near_count)
    rounds = jnp.maximum(
        jnp.floor((most + (cap - 0.5)) / cap), jnp.floor((most_near + (edge_cap - 0.5)) / edge_cap)
    )

    pad = jnp.zeros((LANES - 2 * chunks, LANES), jnp.float32)
    flat = jnp.concatenate([r.astype(jnp.float32), (cl + 1).astype(jnp.float32), pad], axis=0)
    turned = flat.T
    wide[:, :LANES] = x_ref[...]
    for k in range(chunks):
        part = turned if k == 0 else pltpu.roll(turned, LANES - k, 1)
        wide[k * LANES : (k + 1) * LANES, LANES:] = part.astype(jnp.bfloat16)

    per = CHUNK // LANES
    begin = jnp.floor(offset / 8.0) * 8.0
    fits = turn == 0
    spill = jnp.float32(0.0)
    for e, window in enumerate(WINDOWS):
        for s in range(reps):
            lines = slice((2 * s + e) * chunks, (2 * s + e + 1) * chunks)
            worst = ends[lines]
            first_line = begin[lines]
            for j in range(chunks // per):
                room = worst[(j + 1) * per - 1 : (j + 1) * per] - first_line[j * per : j * per + 1]
                spill = jnp.maximum(spill, room - window)
    fits = fits & (jnp.max(spill) <= 0.0) & (jnp.max(most) <= cap)

    @pl.when(fits)
    def _():
        moved[...] = jnp.zeros_like(moved)
        starts = begin.astype(jnp.int32)
        for j in range(chunks // per):
            pieces, spots = [], []
            for s in range(reps):
                for e, window in enumerate(WINDOWS):
                    line = (2 * s + e) * chunks + j * per
                    slot = lax.broadcasted_iota(jnp.int32, (window, LANES), 0).astype(jnp.float32)
                    halves = []
                    for h in range(per):
                        target = place[line + h : line + h + 1] - begin[line : line + 1]
                        halves.append(jnp.where(slot == target, 1.0, 0.0).astype(jnp.bfloat16))
                    pieces.append(jnp.concatenate(halves, axis=1))
                    spots.append((s, window, starts[line, 0]))
            picked = jnp.dot(
                jnp.concatenate(pieces, axis=0),
                wide[j * CHUNK : (j + 1) * CHUNK, :],
                preferred_element_type=jnp.float32,
            )
            at = 0
            for s, window, spot in spots:
                span = pl.ds(pl.multiple_of(spot, 8), window)
                moved[s, span, :] = moved[s, span, :] + picked[at : at + window]
                at += window
        for s in range(reps):
            edge_moved[s] = moved[s, :edge_cap, :]

    @pl.when(jnp.logical_not(fits))
    def _():
        def gather(s, lines, size, out):
            slot = lax.broadcasted_iota(jnp.int32, (size, LANES), 0).astype(jnp.float32)
            slot = slot + (turn * size).astype(jnp.float32)
            for k in range(chunks):
                part = jnp.zeros((size, LANES), jnp.float32)
                for line in lines:
                    row = place[line * chunks + k : line * chunks + k + 1]
                    part = part + jnp.where(slot == row, 1.0, 0.0)
                onehot[:size, k * LANES : (k + 1) * LANES] = part.astype(jnp.bfloat16)
            out[s, :size, :] = jnp.dot(onehot[:size, :], wide[...], preferred_element_type=jnp.float32)

        for s in range(reps):
            gather(s, (2 * s, 2 * s + 1), cap, moved)
            gather(s, (2 * s,), edge_cap, edge_moved)

    pick_row = lax.broadcasted_iota(jnp.int32, (16, LANES), 0)
    pick_lane = lax.broadcasted_iota(jnp.int32, (16, LANES), 1)
    pick = ((pick_row == 0) & (pick_lane == 0)) | ((pick_row == 1) & (pick_lane == chunks))
    pick = jnp.where(pick, 1.0, 0.0).astype(jnp.bfloat16)
    for s in range(reps):
        for size, source, out in ((cap, moved, owns[s]), (edge_cap, edge_moved, edges[s])):
            ready = source[s, :size, :].astype(jnp.bfloat16)
            out[:size, :] = ready[:, :LANES]
            meta = lax.dot_general(
                pick, ready[:, LANES:], (((1,), (1,)), ((), ())), preferred_element_type=jnp.float32
            )
            node_row, node_col = meta[0:1], meta[1:2]
            if out is edges[s]:
                number = lax.broadcasted_iota(jnp.int32, (1, size), 1) + turn * size
                listed = number.astype(jnp.float32) < near_count[s][:, :1]
                node_col = jnp.where(listed, node_col, 0.0)
                node_row = node_row + shift.astype(jnp.float32)
            out[size:, :] = meta_rows(node_row, node_col, rounds, size).astype(jnp.bfloat16)


def meta_rows(node_row, node_col, rounds, cap):
    def split(line):
        parts = []
        for i in range(lane_rows(cap)):
            part = line[:, i * LANES : min((i + 1) * LANES, cap)]
            if part.shape[1] < LANES:
                part = jnp.concatenate([part, jnp.zeros((1, LANES - part.shape[1]), part.dtype)], axis=1)
            parts.append(part)
        return parts

    lines = split(node_col) + split(node_row) + [rounds]
    lines.append(jnp.zeros((META - len(lines), LANES), jnp.float32))
    return jnp.concatenate(lines, axis=0)


def partner_step(me, target, count):
    if count & (count - 1) == 0:
        return lax.bitwise_xor(target, jnp.full(target.shape, me, jnp.int32))
    return lax.rem(target - me + count, count)


def partner(me, step, count):
    return me ^ step if count & (count - 1) == 0 else (me + step) % count


def buckets(vec_rows, index_rows, scal, dims, caps):
    reps = dims[3]
    total = vec_rows.shape[0]
    deep = max(caps) + max(WINDOWS)
    messages = [jax.ShapeDtypeStruct((c + META, LANES), jnp.bfloat16) for c in caps for _ in range(reps)]
    whole = pl.BlockSpec(memory_space=pltpu.VMEM)
    out = pl.pallas_call(
        functools.partial(bucket_kernel, dims, caps),
        out_shape=messages,
        in_specs=[pl.BlockSpec(memory_space=pltpu.SMEM), whole, whole],
        out_specs=[whole] * (2 * reps),
        scratch_shapes=[
            pltpu.VMEM((total, 2 * LANES), jnp.bfloat16),
            pltpu.VMEM((reps, deep, 2 * LANES), jnp.float32),
            pltpu.VMEM((reps, caps[1], 2 * LANES), jnp.float32),
            pltpu.VMEM((max(caps), total), jnp.bfloat16),
        ],
        compiler_params=pltpu.CompilerParams(vmem_limit_bytes=VMEM_LIMIT),
        cost_estimate=pl.CostEstimate(
            flops=2 * reps * 1024 * total * 256, bytes_accessed=2 * total * LANES * 2, transcendentals=0
        ),
        name="buckets",
    )(scal, vec_rows, index_rows)
    return out[:reps], out[reps:]


GROUP = 16


def read_message(message, cap, shape, span):
    rows, cols = shape[0], span[1] - span[0]
    lines = lane_rows(cap)
    width = cap + META
    meta = message[cap:, :].astype(jnp.float32)

    def line(first):
        whole = jnp.concatenate([meta[first + j : first + j + 1] for j in range(lines)], axis=1)[:, :width]
        if whole.shape[1] < width:
            whole = jnp.concatenate([whole, jnp.zeros((1, width - whole.shape[1]), jnp.float32)], axis=1)
        return whole

    node_col, node_row = line(0), line(lines)
    here = lax.broadcasted_iota(jnp.int32, (cols, width), 0).astype(jnp.float32)
    hit = jnp.where(here == node_col - (1.0 + span[0]), 1.0, 0.0).astype(jnp.bfloat16)
    at = lax.broadcasted_iota(jnp.int32, (rows, width), 0).astype(jnp.float32)
    weight = gauss(at - node_row).astype(jnp.bfloat16)
    rounds = jnp.max(meta[2 * lines : 2 * lines + 1])
    return hit, weight, rounds


def weighted(picked, block, message, product):
    count, width = picked.shape
    for i in range(GROUP):
        line = jnp.broadcast_to(block[i : i + 1, :], (count, width)).astype(jnp.bfloat16)
        product[i * count : (i + 1) * count, :width] = picked * line
    total = jnp.dot(product[: GROUP * count, :width], message[...], preferred_element_type=jnp.float32)
    return total.reshape(GROUP, count, LANES)


def sums_kernel(shape, caps, edge_caps, first, *refs):
    rows, cols = shape
    refs = list(refs)
    spot = refs.pop(0) if edge_caps else None
    messages = [refs.pop(0) for _ in caps]
    edges = [refs.pop(0) for _ in edge_caps]
    if not first:
        flag_in, acc_in, cnt_in = refs.pop(0), refs.pop(0), refs.pop(0)
    flag, acc, cnt, weights, product = refs
    counted = jnp.zeros((cols, rows), jnp.float32) if first else cnt_in[...]
    rounds = jnp.float32(0.0)
    chosen = []
    for m, (message, cap) in enumerate(zip(messages + edges, caps + edge_caps)):
        hit, weight, told = read_message(message, cap, shape, (0, cols))
        chosen.append(hit)
        rounds = jnp.maximum(rounds, told)
        weights[m, :, : cap + META] = weight.astype(jnp.float32)
        counted = counted + lax.dot_general(
            hit, weight, (((1,), (1,)), ((), ())), preferred_element_type=jnp.float32
        )
    cnt[...] = counted
    rounds = rounds.astype(jnp.int32)
    flag[0] = rounds if first else jnp.maximum(rounds, flag_in[0])
    for start in range(0, rows, GROUP):
        span = pl.ds(start, GROUP)
        total = jnp.zeros((GROUP, cols, LANES), jnp.float32) if first else acc_in[span]
        for m, message in enumerate(messages):
            total = total + weighted(chosen[m], weights[m, span, : caps[m] + META], message, product)
        acc[span] = total
    if edges:
        span = pl.ds(pl.multiple_of(spot[0], GROUP), GROUP)
        total = acc[span]
        for n, message in enumerate(edges):
            m = len(messages) + n
            total = total + weighted(chosen[m], weights[m, span, : edge_caps[n] + META], message, product)
        acc[span] = total


def sums(messages, edges, spot, state, shape):
    rows, cols = shape
    caps = [m.shape[0] - META for m in messages]
    edge_caps = [m.shape[0] - META for m in edges]
    first = state is None
    smem = pl.BlockSpec(memory_space=pltpu.SMEM)
    whole = pl.BlockSpec(memory_space=pltpu.VMEM)
    specs = [whole] * (len(messages) + len(edges))
    operands = list(messages) + list(edges)
    if edges:
        specs, operands = [smem] + specs, [spot] + operands
    aliases = {}
    if not first:
        aliases = {len(operands) + 1: 1}
        specs += [smem, whole, whole]
        operands += list(state)
    deep = max(caps + edge_caps) + META
    return pl.pallas_call(
        functools.partial(sums_kernel, shape, caps, edge_caps, first),
        out_shape=[
            jax.ShapeDtypeStruct((1,), jnp.int32),
            jax.ShapeDtypeStruct((rows, cols, LANES), jnp.float32),
            jax.ShapeDtypeStruct((cols, rows), jnp.float32),
        ],
        in_specs=specs,
        out_specs=[smem, whole, whole],
        input_output_aliases=aliases,
        scratch_shapes=[
            pltpu.VMEM((len(caps + edge_caps), rows, deep), jnp.float32),
            pltpu.VMEM((GROUP * cols, deep), jnp.bfloat16),
        ],
        compiler_params=pltpu.CompilerParams(vmem_limit_bytes=VMEM_LIMIT),
        cost_estimate=COST,
        name="sums",
    )(*operands)


def border_kernel(shape, message, flag_in, acc, cnt_in, flag, cnt, left, right, weights, product):
    rows, cols = shape
    cap = message.shape[0] - META
    hit, weight, told = read_message(message, cap, shape, (0, cols))
    weights[...] = weight.astype(jnp.float32)
    counted = cnt_in[...] + lax.dot_general(
        hit, weight, (((1,), (1,)), ((), ())), preferred_element_type=jnp.float32
    )
    cnt[...] = counted
    flag[0] = jnp.maximum(told.astype(jnp.int32), flag_in[0])
    fill = [jnp.zeros((cols, LANES - rows), jnp.float32)] if rows < LANES else []
    lane_counts = jnp.concatenate([counted] + fill, axis=1).astype(jnp.bfloat16)
    left[rows : rows + 1] = lane_counts[:HALO][None]
    right[rows : rows + 1] = lane_counts[cols - HALO :][None]
    picked = jnp.concatenate([hit[:HALO], hit[cols - HALO :]], axis=0)
    for start in range(0, rows, GROUP):
        span = pl.ds(start, GROUP)
        total = weighted(picked, weights[span, :], message, product)
        left[span] = (total[:, :HALO] + acc[span, :HALO, :]).astype(jnp.bfloat16)
        right[span] = (total[:, HALO:] + acc[span, cols - HALO :, :]).astype(jnp.bfloat16)


def border(message, state, shape):
    rows, cols = shape
    smem = pl.BlockSpec(memory_space=pltpu.SMEM)
    whole = pl.BlockSpec(memory_space=pltpu.VMEM)
    halo = jax.ShapeDtypeStruct((rows + 1, HALO, LANES), jnp.bfloat16)
    deep = message.shape[0]
    return pl.pallas_call(
        functools.partial(border_kernel, shape),
        out_shape=[
            jax.ShapeDtypeStruct((1,), jnp.int32),
            jax.ShapeDtypeStruct((cols, rows), jnp.float32),
            halo,
            halo,
        ],
        in_specs=[whole, smem, whole, whole],
        out_specs=[smem, whole, whole, whole],
        scratch_shapes=[
            pltpu.VMEM((rows, deep), jnp.float32),
            pltpu.VMEM((GROUP * 2 * HALO, deep), jnp.bfloat16),
        ],
        compiler_params=pltpu.CompilerParams(vmem_limit_bytes=VMEM_LIMIT),
        cost_estimate=COST,
        name="border",
    )(message, *state)


def band_matrix(outs, ins, first_out, first_in, repeat):
    down = lax.broadcasted_iota(jnp.int32, (repeat * outs, repeat * ins), 0)
    across = lax.broadcasted_iota(jnp.int32, (repeat * outs, repeat * ins), 1)
    top, side = quotient(down, outs), quotient(across, ins)
    away = (across - side * ins + first_in) - (down - top * outs + first_out)
    return jnp.where(top == side, gauss(away), 0.0).astype(jnp.bfloat16)


def inner_kernel(shape, message, acc, cnt, left, right, codebook, out, edge, edge_cnt, weights, product, ready, own, sem):
    rows, cols = shape
    cap = message.shape[0] - META
    picked, weight, _ = read_message(message, cap, shape, (HALO, cols - HALO))
    weights[...] = weight.astype(jnp.float32)
    band = band_matrix(cols, cols, 0, 0, 1)
    counted = jnp.dot(band, cnt[...].astype(jnp.bfloat16), preferred_element_type=jnp.float32)
    edge_cnt[:HALO] = counted[:HALO]
    edge_cnt[HALO:] = counted[cols - HALO :]
    scale = 0.7 / (counted[HALO : cols - HALO] + 1.0)
    pair = band_matrix(cols, cols, 0, 0, 2)
    copies = []
    for start in range(0, rows, GROUP):
        span = pl.ds(start, GROUP)
        total = weighted(picked, weights[span, :], message, product)
        own[:, HALO : cols - HALO, :] = (total + acc[span, HALO : cols - HALO, :]).astype(jnp.bfloat16)
        own[:, :HALO, :] = left[span]
        own[:, cols - HALO :, :] = right[span]
        for i in range(0, GROUP, 4):
            sides = [jnp.concatenate([own[i + 2 * j], own[i + 2 * j + 1]], axis=0) for j in range(2)]
            smooth = jnp.dot(pair, jnp.concatenate(sides, axis=1), preferred_element_type=jnp.float32)
            for j in range(4):
                a = start + i + j
                mine = smooth[(j % 2) * cols : (j % 2 + 1) * cols, (j // 2) * LANES : (j // 2 + 1) * LANES]
                edge[a, :HALO, :] = mine[:HALO]
                edge[a, HALO:, :] = mine[cols - HALO :]
                old = codebook[a, HALO : cols - HALO, :].astype(jnp.float32)
                fresh = 0.3 * old + mine[HALO : cols - HALO] * scale[:, a : a + 1]
                ready[a] = fresh.astype(jnp.bfloat16)
        copies.append(
            pltpu.make_async_copy(ready.at[span], out.at[span, HALO : cols - HALO, :], sem.at[start // GROUP])
        )
        copies[-1].start()
    for copy in copies:
        copy.wait()


def outer_kernel(shape, from_left, from_right, edge, edge_cnt, codebook, inner, out, ready, sem):
    rows, cols = shape
    del inner
    eight = LANES // HALO
    copies = []
    for side, halo in enumerate((from_left, from_right)):
        first_out, first_in = ((0, -HALO), (cols - HALO, cols))[side]
        columns = slice(first_out, first_out + HALO)
        band = band_matrix(HALO, HALO, first_out, first_in, 1)
        counted = jnp.dot(band, halo[rows], preferred_element_type=jnp.float32)[:, :rows]
        counted = counted + edge_cnt[side * HALO : (side + 1) * HALO]
        scale = 0.7 / (counted + 1.0)
        blocks = band_matrix(HALO, HALO, first_out, first_in, eight)
        for start in range(0, rows, 2 * eight):
            there = [
                halo[start + j * eight : start + (j + 1) * eight].reshape(LANES, LANES) for j in range(2)
            ]
            smooth = jnp.dot(blocks, jnp.concatenate(there, axis=1), preferred_element_type=jnp.float32)
            for j in range(2 * eight):
                a = start + j
                top, lane = (j % eight) * HALO, (j // eight) * LANES
                mine = smooth[top : top + HALO, lane : lane + LANES]
                mine = mine + edge[a, side * HALO : (side + 1) * HALO, :]
                fresh = 0.3 * codebook[a, columns, :].astype(jnp.float32) + mine * scale[:, a : a + 1]
                ready[side, a] = fresh.astype(jnp.bfloat16)
        copies.append(pltpu.make_async_copy(ready.at[side], out.at[:, columns, :], sem.at[side]))
        copies[-1].start()
    for copy in copies:
        copy.wait()


def inner_mix(message, acc, cnt, left, right, codebook):
    rows, cols, width = codebook.shape
    whole = pl.BlockSpec(memory_space=pltpu.VMEM)
    deep = message.shape[0]
    middle = cols - 2 * HALO
    return pl.pallas_call(
        functools.partial(inner_kernel, (rows, cols)),
        out_shape=[
            jax.ShapeDtypeStruct(codebook.shape, jnp.bfloat16),
            jax.ShapeDtypeStruct((rows, 2 * HALO, width), jnp.float32),
            jax.ShapeDtypeStruct((2 * HALO, rows), jnp.float32),
        ],
        in_specs=[whole] * 6,
        out_specs=[pl.BlockSpec(memory_space=pl.ANY), whole, whole],
        scratch_shapes=[
            pltpu.VMEM((rows, deep), jnp.float32),
            pltpu.VMEM((GROUP * middle, deep), jnp.bfloat16),
            pltpu.VMEM((rows, middle, width), jnp.bfloat16),
            pltpu.VMEM((GROUP, cols, width), jnp.bfloat16),
            pltpu.SemaphoreType.DMA((rows // GROUP,)),
        ],
        compiler_params=pltpu.CompilerParams(vmem_limit_bytes=VMEM_LIMIT),
        cost_estimate=COST,
        name="inner",
    )(message, acc, cnt, left, right, codebook)


def outer_mix(from_left, from_right, edge, edge_cnt, codebook, inner):
    rows, cols, width = codebook.shape
    whole = pl.BlockSpec(memory_space=pltpu.VMEM)
    anywhere = pl.BlockSpec(memory_space=pl.ANY)
    return pl.pallas_call(
        functools.partial(outer_kernel, (rows, cols)),
        out_shape=jax.ShapeDtypeStruct(codebook.shape, jnp.bfloat16),
        in_specs=[whole] * 5 + [anywhere],
        out_specs=anywhere,
        input_output_aliases={5: 0},
        scratch_shapes=[
            pltpu.VMEM((2, rows, HALO, width), jnp.bfloat16),
            pltpu.SemaphoreType.DMA((2,)),
        ],
        compiler_params=pltpu.CompilerParams(vmem_limit_bytes=VMEM_LIMIT),
        name="outer",
    )(from_left, from_right, edge, edge_cnt, codebook, inner)


def body(vectors, best_node, codebook):
    rows, cols, width = codebook.shape
    reps, bands = lax.axis_size("rep"), lax.axis_size("row")
    dims = (rows, cols * reps, cols, reps)
    shape = (rows, cols)
    vec_rows = vectors.reshape(-1, width)
    total = vec_rows.shape[0]
    index_rows = best_node.reshape(-1, LANES)
    me, band = lax.axis_index("rep"), lax.axis_index("row")
    cap = capacity(total, 1.0 / reps)
    edge_cap = capacity(total, RADIUS / rows / reps)
    zero = jnp.int32(0)

    if bands == 2:
        up = band == 0
        low = jnp.where(up, rows - RADIUS, 0)
        sides = [
            ([(0, 1), (1, 0)], jnp.where(up, -rows, rows), low, low + RADIUS, jnp.where(up, rows - GROUP, 0))
        ]
    else:
        sides = [
            ([(i, i + 1) for i in range(bands - 1)], -rows, rows - RADIUS, rows, 0),
            ([(i + 1, i) for i in range(bands - 1)], rows, 0, RADIUS, rows - GROUP),
        ]

    def send_own(own):
        return [
            lax.ppermute(own[s], "rep", [(i, partner(i, s, reps)) for i in range(reps)])
            for s in range(1, reps)
        ]

    def send_edges(near, pairs):
        return [
            lax.ppermute(
                message,
                ("row", "rep"),
                [(a * reps + i, b * reps + partner(i, s, reps)) for a, b in pairs for i in range(reps)],
            )
            for s, message in enumerate(near)
        ]

    def one_round(state, turn, skip):
        nears = []
        for pairs, shift, low, high, touched in sides:
            scal = jnp.stack([me, turn, jnp.int32(shift), jnp.int32(low), jnp.int32(high)])
            own, near = buckets(vec_rows, index_rows, scal, dims, (cap, edge_cap))
            if not nears:
                mine = own
            nears.append((near, jnp.reshape(jnp.int32(touched), (1,))))
        ways = [side[0] for side in sides]
        arrived = send_own(mine)
        state = sums([mine[0]], [], None, state, shape)
        nears, state = lax.optimization_barrier((nears, state)) if ORDER else (nears, state)
        edges = [(send_edges(near, pairs), touched) for (near, touched), pairs in zip(nears, ways)]
        late = arrived.pop()
        for n, message in enumerate(arrived):
            for side in edges[1:] if n == 0 else []:
                state = sums([message], *side, state, shape)
                break
            else:
                side = edges[0] if n == len(arrived) - 1 else ([], None)
                state = sums([message], *side, state, shape)
        return (state, late) if skip else sums([late], [], None, state, shape)

    def agreed(flag):
        return flag if bands == 2 else lax.pmax(flag, ("row", "rep"))

    (flag, acc, cnt), last = one_round(None, zero, True)
    flag, full_cnt, left, right = border(last, (flag, acc, cnt), shape)

    def more(carry):
        return carry[0] < carry[1][0]

    def again(carry):
        turn, flag, acc, cnt, full_cnt, left, right = carry
        flag, acc, cnt = one_round((flag, acc, cnt), turn, False)
        flag, full_cnt, left, right = border(last, (flag, acc, cnt), shape)
        return turn + 1, agreed(flag), acc, cnt, full_cnt, left, right

    _, _, acc, _, cnt, left, right = lax.while_loop(
        more, again, (jnp.int32(1), agreed(flag), acc, cnt, full_cnt, left, right)
    )
    peers = lax.axis_size(("col", "rep"))
    from_left = lax.ppermute(right, ("col", "rep"), [(i, i + 1) for i in range(peers - 1)])
    from_right = lax.ppermute(left, ("col", "rep"), [(i + 1, i) for i in range(peers - 1)])
    inner, edge, edge_cnt = inner_mix(last, acc, cnt, left, right, codebook)
    return outer_mix(from_left, from_right, edge, edge_cnt, codebook, inner)


def solution(mesh):
    placed = (P("row", "col", "rep", None), P("row", "col", "rep"), P("row", ("col", "rep"), None))
    return jax.shard_map(
        body, mesh=mesh, in_specs=placed, out_specs=P("row", ("col", "rep"), None), check_vma=False
    )
```

```python
import functools
import math

import jax
import jax.numpy as jnp
from jax import lax
from jax.experimental import pallas as pl
from jax.experimental.pallas import tpu as pltpu
from jax.sharding import PartitionSpec as P

RADIUS = 15
LANES = 128
META = 16
HALO = 16
GROUP = 16
STATUS = 8
VMEM_LIMIT = 24 * 1024 * 1024
COST = pl.CostEstimate(flops=2**20, bytes_accessed=2**16, transcendentals=0)


def gauss(distance):
    d = distance.astype(jnp.float32)
    weight = jnp.exp(-(d * d) / (2.0 * RADIUS * RADIUS))
    return jnp.where(jnp.abs(d) <= RADIUS, weight, 0.0)


def capacity(total, share):
    mean = total * share
    spread = math.sqrt(total * share * (1.0 - share))
    return min(-(-int(mean + 4.7 * spread) // 16) * 16, -(-total // 16) * 16)


def quotient(value, by):
    if by & (by - 1) == 0:
        return lax.shift_right_logical(value, by.bit_length() - 1)
    return lax.div(value, by)


def lane_rows(total):
    return -(-total // LANES)


def side_of(side, rows):
    if side == "next":
        return jnp.int32(-rows), jnp.int32(rows - RADIUS), jnp.int32(0)
    if side == "previous":
        return jnp.int32(rows), jnp.int32(0), jnp.int32(rows - GROUP)
    top = lax.axis_index("row") == 0
    there = [jnp.where(top, a, b) for a, b in ((-rows, rows), (rows - RADIUS, 0), (rows - GROUP, 0))]
    return tuple(there)


CHUNK = 256
WINDOWS = (48, 96)


def bucket_kernel(dims, caps, side, turn_ref, x_ref, idx_ref, *rest):
    rows, block_cols, cols, reps = dims
    cap, edge_cap = caps
    owns, edges = rest[:reps], rest[reps : 2 * reps]
    wide, moved, edge_moved, onehot = rest[2 * reps :]
    me, turn = lax.axis_index("rep"), turn_ref[0]
    shift, low, _ = side_of(side, rows)
    high = low + RADIUS
    idx = idx_ref[...]
    chunks = idx.shape[0]
    r = quotient(idx, block_cols)
    c = idx - r * block_cols
    t = quotient(c, cols)
    cl = c - t * cols
    step = partner_step(me, t, reps)
    near = (r >= low) & (r < high)
    member = []
    for s in range(reps):
        here = step == s
        member += [here & near, here & jnp.logical_not(near)]
    members = jnp.concatenate([jnp.where(m, 1.0, 0.0) for m in member], axis=0)
    members16 = members.astype(jnp.bfloat16)
    count = 2 * reps * chunks
    up = lax.broadcasted_iota(jnp.int32, (LANES, LANES), 0)
    across = lax.broadcasted_iota(jnp.int32, (LANES, LANES), 1)
    tri = jnp.where(up <= across, 1.0, 0.0).astype(jnp.bfloat16)
    ones = jnp.ones((LANES, LANES), jnp.bfloat16)
    both = jnp.concatenate([tri, ones], axis=1)
    scanned = jnp.dot(members16, both, preferred_element_type=jnp.float32)
    inside, totals = scanned[:, :LANES], scanned[:, LANES:]
    i0 = lax.broadcasted_iota(jnp.int32, (count, count), 0)
    i1 = lax.broadcasted_iota(jnp.int32, (count, count), 1)
    group = 2 * chunks
    before = (quotient(i0, group) == quotient(i1, group)) & (i1 < i0)
    before = jnp.where(before, 1.0, 0.0).astype(jnp.bfloat16)
    offset = jnp.dot(before, totals.astype(jnp.bfloat16), preferred_element_type=jnp.float32)
    place = jnp.where(members > 0.5, offset + inside - 1.0, -1.0)
    ends = offset + totals
    near_count = [ends[s * group + chunks - 1 : s * group + chunks] for s in range(reps)]
    own_count = [ends[(s + 1) * group - 1 : (s + 1) * group] for s in range(reps)]
    most = functools.reduce(jnp.maximum, own_count)
    most_near = functools.reduce(jnp.maximum, near_count)
    rounds = jnp.maximum(
        jnp.floor((most + (cap - 0.5)) / cap), jnp.floor((most_near + (edge_cap - 0.5)) / edge_cap)
    )

    pad = jnp.zeros((LANES - 2 * chunks, LANES), jnp.float32)
    flat = jnp.concatenate([r.astype(jnp.float32), (cl + 1).astype(jnp.float32), pad], axis=0)
    turned = flat.T
    wide[:, :LANES] = x_ref[...]
    for k in range(chunks):
        part = turned if k == 0 else pltpu.roll(turned, LANES - k, 1)
        wide[k * LANES : (k + 1) * LANES, LANES:] = part.astype(jnp.bfloat16)

    per = CHUNK // LANES
    begin = jnp.floor(offset / 8.0) * 8.0
    fits = turn == 0
    spill = jnp.float32(0.0)
    for e, window in enumerate(WINDOWS):
        for s in range(reps):
            lines = slice((2 * s + e) * chunks, (2 * s + e + 1) * chunks)
            worst = ends[lines]
            first_line = begin[lines]
            for j in range(chunks // per):
                room = worst[(j + 1) * per - 1 : (j + 1) * per] - first_line[j * per : j * per + 1]
                spill = jnp.maximum(spill, room - window)
    fits = fits & (jnp.max(spill) <= 0.0) & (jnp.max(most) <= cap)

    @pl.when(fits)
    def _():
        moved[...] = jnp.zeros_like(moved)
        starts = begin.astype(jnp.int32)
        for j in range(chunks // per):
            pieces, spots = [], []
            for s in range(reps):
                for e, window in enumerate(WINDOWS):
                    line = (2 * s + e) * chunks + j * per
                    slot = lax.broadcasted_iota(jnp.int32, (window, LANES), 0).astype(jnp.float32)
                    halves = []
                    for h in range(per):
                        target = place[line + h : line + h + 1] - begin[line : line + 1]
                        halves.append(jnp.where(slot == target, 1.0, 0.0).astype(jnp.bfloat16))
                    pieces.append(jnp.concatenate(halves, axis=1))
                    spots.append((s, window, starts[line, 0]))
            picked = jnp.dot(
                jnp.concatenate(pieces, axis=0),
                wide[j * CHUNK : (j + 1) * CHUNK, :],
                preferred_element_type=jnp.float32,
            )
            at = 0
            for s, window, spot in spots:
                span = pl.ds(pl.multiple_of(spot, 8), window)
                moved[s, span, :] = moved[s, span, :] + picked[at : at + window]
                at += window
        for s in range(reps):
            edge_moved[s] = moved[s, :edge_cap, :]

    @pl.when(jnp.logical_not(fits))
    def _():
        def gather(s, lines, size, out):
            slot = lax.broadcasted_iota(jnp.int32, (size, LANES), 0).astype(jnp.float32)
            slot = slot + (turn * size).astype(jnp.float32)
            for k in range(chunks):
                part = jnp.zeros((size, LANES), jnp.float32)
                for line in lines:
                    row = place[line * chunks + k : line * chunks + k + 1]
                    part = part + jnp.where(slot == row, 1.0, 0.0)
                onehot[:size, k * LANES : (k + 1) * LANES] = part.astype(jnp.bfloat16)
            out[s, :size, :] = jnp.dot(onehot[:size, :], wide[...], preferred_element_type=jnp.float32)

        for s in range(reps):
            gather(s, (2 * s, 2 * s + 1), cap, moved)
            gather(s, (2 * s,), edge_cap, edge_moved)

    pick_row = lax.broadcasted_iota(jnp.int32, (16, LANES), 0)
    pick_lane = lax.broadcasted_iota(jnp.int32, (16, LANES), 1)
    pick = ((pick_row == 0) & (pick_lane == 0)) | ((pick_row == 1) & (pick_lane == chunks))
    pick = jnp.where(pick, 1.0, 0.0).astype(jnp.bfloat16)
    for s in range(reps):
        for size, source, out in ((cap, moved, owns[s]), (edge_cap, edge_moved, edges[s])):
            ready = source[s, :size, :].astype(jnp.bfloat16)
            out[:size, :] = ready[:, :LANES]
            meta = lax.dot_general(
                pick, ready[:, LANES:], (((1,), (1,)), ((), ())), preferred_element_type=jnp.float32
            )
            node_row, node_col = meta[0:1], meta[1:2]
            if out is edges[s]:
                number = lax.broadcasted_iota(jnp.int32, (1, size), 1) + turn * size
                listed = number.astype(jnp.float32) < near_count[s][:, :1]
                node_col = jnp.where(listed, node_col, 0.0)
                node_row = node_row + shift.astype(jnp.float32)
            out[size:, :] = meta_rows(node_row, node_col, rounds, size).astype(jnp.bfloat16)


def meta_rows(node_row, node_col, rounds, cap):
    def split(line):
        parts = []
        for i in range(lane_rows(cap)):
            part = line[:, i * LANES : min((i + 1) * LANES, cap)]
            if part.shape[1] < LANES:
                part = jnp.concatenate([part, jnp.zeros((1, LANES - part.shape[1]), part.dtype)], axis=1)
            parts.append(part)
        return parts

    lines = split(node_col) + split(node_row) + [rounds]
    lines.append(jnp.zeros((META - len(lines), LANES), jnp.float32))
    return jnp.concatenate(lines, axis=0)


def partner_step(me, target, count):
    if count & (count - 1) == 0:
        return lax.bitwise_xor(target, jnp.full(target.shape, me, jnp.int32))
    return lax.rem(target - me + count, count)


def partner(me, step, count):
    return me ^ step if count & (count - 1) == 0 else (me + step) % count


def buckets(vec_rows, index_rows, turn, dims, caps, side):
    reps = dims[3]
    total = vec_rows.shape[0]
    deep = max(caps) + max(WINDOWS)
    messages = [jax.ShapeDtypeStruct((c + META, LANES), jnp.bfloat16) for c in caps for _ in range(reps)]
    whole = pl.BlockSpec(memory_space=pltpu.VMEM)
    out = pl.pallas_call(
        functools.partial(bucket_kernel, dims, caps, side),
        out_shape=messages,
        in_specs=[pl.BlockSpec(memory_space=pltpu.SMEM), whole, whole],
        out_specs=[whole] * (2 * reps),
        scratch_shapes=[
            pltpu.VMEM((total, 2 * LANES), jnp.bfloat16),
            pltpu.VMEM((reps, deep, 2 * LANES), jnp.float32),
            pltpu.VMEM((reps, caps[1], 2 * LANES), jnp.float32),
            pltpu.VMEM((max(caps), total), jnp.bfloat16),
        ],
        compiler_params=pltpu.CompilerParams(vmem_limit_bytes=VMEM_LIMIT),
        cost_estimate=pl.CostEstimate(
            flops=2 * reps * 1024 * total * 256, bytes_accessed=2 * total * LANES * 2, transcendentals=0
        ),
        name="buckets",
    )(turn, vec_rows, index_rows)
    return out[:reps], out[reps:]


def read_message(message, cap, shape, span):
    rows, cols = shape[0], span[1] - span[0]
    lines = lane_rows(cap)
    width = cap + META
    meta = message[cap:, :].astype(jnp.float32)

    def line(first):
        whole = jnp.concatenate([meta[first + j : first + j + 1] for j in range(lines)], axis=1)[:, :width]
        if whole.shape[1] < width:
            whole = jnp.concatenate([whole, jnp.zeros((1, width - whole.shape[1]), jnp.float32)], axis=1)
        return whole

    node_col, node_row = line(0), line(lines)
    here = lax.broadcasted_iota(jnp.int32, (cols, width), 0).astype(jnp.float32)
    hit = jnp.where(here == node_col - (1.0 + span[0]), 1.0, 0.0).astype(jnp.bfloat16)
    at = lax.broadcasted_iota(jnp.int32, (rows, width), 0).astype(jnp.float32)
    weight = gauss(at - node_row).astype(jnp.bfloat16)
    rounds = jnp.max(meta[2 * lines : 2 * lines + 1])
    return hit, weight, rounds


def weighted(picked, block, message, product):
    count, width = picked.shape
    for i in range(GROUP):
        line = jnp.broadcast_to(block[i : i + 1, :], (count, width)).astype(jnp.bfloat16)
        product[i * count : (i + 1) * count, :width] = picked * line
    total = jnp.dot(product[: GROUP * count, :width], message[...], preferred_element_type=jnp.float32)
    return total.reshape(GROUP, count, LANES)


def edge_sums(sides, names, caps, shape, pieces, weights, product, counted):
    results, rounds = [], jnp.float32(0.0)
    for n, messages in enumerate(sides):
        span = pl.ds(pl.multiple_of(side_of(names[n], shape[0])[2], GROUP), GROUP)
        total = None
        for message, cap in zip(messages, caps[n]):
            hits = []
            for piece in pieces:
                hit, weight, told = read_message(message, cap, shape, piece)
                hits.append(hit)
            rounds = jnp.maximum(rounds, told)
            weights[:, : cap + META] = weight.astype(jnp.float32)
            if counted is not None:
                hit, _, _ = read_message(message, cap, shape, (0, shape[1]))
                counted = counted + count_nodes(hit, weight)
            hits = hits[0] if len(hits) == 1 else jnp.concatenate(hits, axis=0)
            term = weighted(hits, weights[span, : cap + META], message, product)
            total = term if total is None else total + term
        results.append((span, total))
    return results, rounds, counted


def count_nodes(hit, weight):
    return lax.dot_general(hit, weight, (((1,), (1,)), ((), ())), preferred_element_type=jnp.float32)


def split_sides(refs, counts):
    return [[refs.pop(0) for _ in range(count)] for count in counts]


def sums_kernel(shape, caps, names, side_caps, first, *refs):
    rows, cols = shape
    refs = list(refs)
    messages = [refs.pop(0) for _ in caps]
    sides = split_sides(refs, [len(c) for c in side_caps])
    if not first:
        acc_in, cnt_in = refs.pop(0), refs.pop(0)
    acc, cnt, weights, edge_weights, product = refs
    counted = jnp.zeros((cols, rows), jnp.float32) if first else cnt_in[:cols]
    rounds = jnp.zeros((STATUS, rows), jnp.float32) if first else cnt_in[cols:]
    chosen = []
    for m, (message, cap) in enumerate(zip(messages, caps)):
        hit, weight, told = read_message(message, cap, shape, (0, cols))
        chosen.append(hit)
        rounds = jnp.maximum(rounds, told)
        weights[m, :, : cap + META] = weight.astype(jnp.float32)
        counted = counted + count_nodes(hit, weight)
    for start in range(0, rows, GROUP):
        span = pl.ds(start, GROUP)
        total = jnp.zeros((GROUP, cols, LANES), jnp.float32) if first else acc_in[span]
        for m, message in enumerate(messages):
            total = total + weighted(chosen[m], weights[m, span, : caps[m] + META], message, product)
        acc[span] = total
    if sides:
        totals, told, counted = edge_sums(
            sides, names, side_caps, shape, [(0, cols)], edge_weights, product, counted
        )
        rounds = jnp.maximum(rounds, told)
        for span, total in totals:
            acc[span] = acc[span] + total
    cnt[:cols] = counted
    cnt[cols:] = rounds


def sums(messages, sides, names, state, shape):
    rows, cols = shape
    caps = [m.shape[0] - META for m in messages]
    side_caps = [[m.shape[0] - META for m in side] for side in sides]
    first = state is None
    whole = pl.BlockSpec(memory_space=pltpu.VMEM)
    operands = list(messages) + [m for side in sides for m in side]
    specs = [whole] * len(operands)
    aliases = {}
    if not first:
        aliases = {len(operands): 0, len(operands) + 1: 1}
        specs += [whole, whole]
        operands += list(state)
    deep = max(caps) + META
    return pl.pallas_call(
        functools.partial(sums_kernel, shape, caps, names, side_caps, first),
        out_shape=[
            jax.ShapeDtypeStruct((rows, cols, LANES), jnp.float32),
            jax.ShapeDtypeStruct((cols + STATUS, rows), jnp.float32),
        ],
        in_specs=specs,
        out_specs=[whole, whole],
        input_output_aliases=aliases,
        scratch_shapes=[
            pltpu.VMEM((len(caps), rows, deep), jnp.float32),
            pltpu.VMEM((rows, deep), jnp.float32),
            pltpu.VMEM((GROUP * cols, deep), jnp.bfloat16),
        ],
        compiler_params=pltpu.CompilerParams(vmem_limit_bytes=VMEM_LIMIT),
        cost_estimate=COST,
        name="sums",
    )(*operands)


def border_kernel(shape, names, side_caps, *refs):
    rows, cols = shape
    refs = list(refs)
    sides = split_sides(refs, [len(c) for c in side_caps])
    acc, cnt_in, flag, cnt, left, right, weights, product = refs
    left[:rows] = acc[:, :HALO, :].astype(jnp.bfloat16)
    right[:rows] = acc[:, cols - HALO :, :].astype(jnp.bfloat16)
    totals, told, counted = edge_sums(
        sides, names, side_caps, shape, [(0, HALO), (cols - HALO, cols)], weights, product, cnt_in[:cols]
    )
    for span, total in totals:
        left[span] = (total[:, :HALO] + acc[span, :HALO, :]).astype(jnp.bfloat16)
        right[span] = (total[:, HALO:] + acc[span, cols - HALO :, :]).astype(jnp.bfloat16)
    cnt[...] = counted
    flag[0] = jnp.max(jnp.maximum(told, cnt_in[cols:])).astype(jnp.int32)
    fill = [jnp.zeros((cols, LANES - rows), jnp.float32)] if rows < LANES else []
    lane_counts = jnp.concatenate([counted] + fill, axis=1).astype(jnp.bfloat16)
    left[rows : rows + 1] = lane_counts[:HALO][None]
    right[rows : rows + 1] = lane_counts[cols - HALO :][None]


def border(sides, names, state, shape):
    rows, cols = shape
    smem = pl.BlockSpec(memory_space=pltpu.SMEM)
    whole = pl.BlockSpec(memory_space=pltpu.VMEM)
    halo = jax.ShapeDtypeStruct((rows + 1, HALO, LANES), jnp.bfloat16)
    edges = [m for side in sides for m in side]
    side_caps = [[m.shape[0] - META for m in side] for side in sides]
    deep = edges[0].shape[0]
    return pl.pallas_call(
        functools.partial(border_kernel, shape, names, side_caps),
        out_shape=[
            jax.ShapeDtypeStruct((1,), jnp.int32),
            jax.ShapeDtypeStruct((cols, rows), jnp.float32),
            halo,
            halo,
        ],
        in_specs=[whole] * (len(edges) + 2),
        out_specs=[smem, whole, whole, whole],
        scratch_shapes=[
            pltpu.VMEM((rows, deep), jnp.float32),
            pltpu.VMEM((GROUP * 2 * HALO, deep), jnp.bfloat16),
        ],
        compiler_params=pltpu.CompilerParams(vmem_limit_bytes=VMEM_LIMIT),
        cost_estimate=COST,
        name="border",
    )(*edges, *state)


def band_matrix(outs, ins, first_out, first_in, repeat):
    down = lax.broadcasted_iota(jnp.int32, (repeat * outs, repeat * ins), 0)
    across = lax.broadcasted_iota(jnp.int32, (repeat * outs, repeat * ins), 1)
    top, side = quotient(down, outs), quotient(across, ins)
    away = (across - side * ins + first_in) - (down - top * outs + first_out)
    return jnp.where(top == side, gauss(away), 0.0).astype(jnp.bfloat16)


def inner_kernel(shape, names, side_caps, *refs):
    rows, cols = shape
    refs = list(refs)
    sides = split_sides(refs, [len(c) for c in side_caps])
    acc, cnt, left, right, codebook, out, edge, edge_cnt, weights, product, ready, own, sem = refs
    middle = slice(HALO, cols - HALO)
    own[:, middle, :] = acc[:, middle, :].astype(jnp.bfloat16)
    own[:, :HALO, :] = left[:rows]
    own[:, cols - HALO :, :] = right[:rows]
    totals, _, _ = edge_sums(sides, names, side_caps, shape, [(HALO, cols - HALO)], weights, product, None)
    for span, total in totals:
        own[span, middle, :] = (total + acc[span, middle, :]).astype(jnp.bfloat16)
    band = band_matrix(cols, cols, 0, 0, 1)
    counted = jnp.dot(band, cnt[...].astype(jnp.bfloat16), preferred_element_type=jnp.float32)
    edge_cnt[:HALO] = counted[:HALO]
    edge_cnt[HALO:] = counted[cols - HALO :]
    scale = 0.7 / (counted[HALO : cols - HALO] + 1.0)
    pair = band_matrix(cols, cols, 0, 0, 2)
    copies = []
    for start in range(0, rows, GROUP):
        span = pl.ds(start, GROUP)
        for i in range(start, start + GROUP, 4):
            twos = [jnp.concatenate([own[i + 2 * j], own[i + 2 * j + 1]], axis=0) for j in range(2)]
            smooth = jnp.dot(pair, jnp.concatenate(twos, axis=1), preferred_element_type=jnp.float32)
            for j in range(4):
                a = i + j
                mine = smooth[(j % 2) * cols : (j % 2 + 1) * cols, (j // 2) * LANES : (j // 2 + 1) * LANES]
                edge[a, :HALO, :] = mine[:HALO]
                edge[a, HALO:, :] = mine[cols - HALO :]
                old = codebook[a, HALO : cols - HALO, :].astype(jnp.float32)
                fresh = 0.3 * old + mine[HALO : cols - HALO] * scale[:, a : a + 1]
                ready[a] = fresh.astype(jnp.bfloat16)
        copies.append(
            pltpu.make_async_copy(ready.at[span], out.at[span, HALO : cols - HALO, :], sem.at[start // GROUP])
        )
        copies[-1].start()
    for copy in copies:
        copy.wait()


def outer_kernel(shape, from_left, from_right, edge, edge_cnt, codebook, inner, out, ready, sem):
    rows, cols = shape
    del inner
    eight = LANES // HALO
    copies = []
    for side, halo in enumerate((from_left, from_right)):
        first_out, first_in = ((0, -HALO), (cols - HALO, cols))[side]
        columns = slice(first_out, first_out + HALO)
        band = band_matrix(HALO, HALO, first_out, first_in, 1)
        counted = jnp.dot(band, halo[rows], preferred_element_type=jnp.float32)[:, :rows]
        counted = counted + edge_cnt[side * HALO : (side + 1) * HALO]
        scale = 0.7 / (counted + 1.0)
        blocks = band_matrix(HALO, HALO, first_out, first_in, eight)
        for step, start in enumerate(range(0, rows, 2 * eight)):
            there = [
                halo[start + j * eight : start + (j + 1) * eight].reshape(LANES, LANES) for j in range(2)
            ]
            smooth = jnp.dot(blocks, jnp.concatenate(there, axis=1), preferred_element_type=jnp.float32)
            for j in range(2 * eight):
                a = start + j
                top, lane = (j % eight) * HALO, (j // eight) * LANES
                mine = smooth[top : top + HALO, lane : lane + LANES]
                mine = mine + edge[a, side * HALO : (side + 1) * HALO, :]
                fresh = 0.3 * codebook[a, columns, :].astype(jnp.float32) + mine * scale[:, a : a + 1]
                ready[side, a] = fresh.astype(jnp.bfloat16)
            span = pl.ds(start, 2 * eight)
            copies.append(
                pltpu.make_async_copy(ready.at[side, span], out.at[span, columns, :], sem.at[side, step])
            )
            copies[-1].start()
    for copy in copies:
        copy.wait()


def inner_mix(sides, names, acc, cnt, left, right, codebook):
    rows, cols, width = codebook.shape
    whole = pl.BlockSpec(memory_space=pltpu.VMEM)
    edges = [m for side in sides for m in side]
    side_caps = [[m.shape[0] - META for m in side] for side in sides]
    deep = edges[0].shape[0]
    middle = cols - 2 * HALO
    return pl.pallas_call(
        functools.partial(inner_kernel, (rows, cols), names, side_caps),
        out_shape=[
            jax.ShapeDtypeStruct(codebook.shape, jnp.bfloat16),
            jax.ShapeDtypeStruct((rows, 2 * HALO, width), jnp.float32),
            jax.ShapeDtypeStruct((2 * HALO, rows), jnp.float32),
        ],
        in_specs=[whole] * (len(edges) + 5),
        out_specs=[pl.BlockSpec(memory_space=pl.ANY), whole, whole],
        scratch_shapes=[
            pltpu.VMEM((rows, deep), jnp.float32),
            pltpu.VMEM((GROUP * middle, deep), jnp.bfloat16),
            pltpu.VMEM((rows, middle, width), jnp.bfloat16),
            pltpu.VMEM((rows, cols, width), jnp.bfloat16),
            pltpu.SemaphoreType.DMA((rows // GROUP,)),
        ],
        compiler_params=pltpu.CompilerParams(vmem_limit_bytes=VMEM_LIMIT),
        cost_estimate=COST,
        name="inner",
    )(*edges, acc, cnt, left, right, codebook)


def outer_mix(from_left, from_right, edge, edge_cnt, codebook, inner):
    rows, cols, width = codebook.shape
    whole = pl.BlockSpec(memory_space=pltpu.VMEM)
    anywhere = pl.BlockSpec(memory_space=pl.ANY)
    return pl.pallas_call(
        functools.partial(outer_kernel, (rows, cols)),
        out_shape=jax.ShapeDtypeStruct(codebook.shape, jnp.bfloat16),
        in_specs=[whole] * 5 + [anywhere],
        out_specs=anywhere,
        input_output_aliases={5: 0},
        scratch_shapes=[
            pltpu.VMEM((2, rows, HALO, width), jnp.bfloat16),
            pltpu.SemaphoreType.DMA((2, rows * HALO // (2 * LANES))),
        ],
        compiler_params=pltpu.CompilerParams(vmem_limit_bytes=VMEM_LIMIT),
        name="outer",
    )(from_left, from_right, edge, edge_cnt, codebook, inner)


def body(vectors, best_node, codebook):
    rows, cols, width = codebook.shape
    reps, bands = lax.axis_size("rep"), lax.axis_size("row")
    dims = (rows, cols * reps, cols, reps)
    shape = (rows, cols)
    vec_rows = vectors.reshape(-1, width)
    total = vec_rows.shape[0]
    index_rows = best_node.reshape(-1, LANES)
    cap = capacity(total, 1.0 / reps)
    edge_cap = capacity(total, RADIUS / rows / reps)

    if bands == 2:
        sides = {"other": [(0, 1), (1, 0)]}
    else:
        sides = {
            "next": [(i, i + 1) for i in range(bands - 1)],
            "previous": [(i + 1, i) for i in range(bands - 1)],
        }
    names = list(sides)

    def send_own(own):
        return [
            lax.ppermute(own[s], "rep", [(i, partner(i, s, reps)) for i in range(reps)])
            for s in range(1, reps)
        ]

    def send_edges(near, pairs, ahead):
        arrived = []
        for s, message in enumerate(near):
            if s >= ahead:
                message, arrived[s - ahead] = lax.optimization_barrier((message, arrived[s - ahead]))
            joint = [(a * reps + i, b * reps + partner(i, s, reps)) for a, b in pairs for i in range(reps)]
            arrived.append(lax.ppermute(message, ("row", "rep"), joint))
        return arrived

    def one_round(state, turn):
        near = []
        for name in names:
            own, edge = buckets(vec_rows, index_rows, jnp.reshape(turn, (1,)), dims, (cap, edge_cap), name)
            mine = mine if near else own
            near.append(edge)
        arrived = send_own(mine)
        state = sums([mine[0]], [], names, state, shape)
        near, state = lax.optimization_barrier((near, state))
        edges = [send_edges(edge, sides[name], 2) for edge, name in zip(near, names)]
        for message in arrived:
            state = sums([message], [], names, state, shape)
        return state, edges

    def late_edges(edges, state):
        none = jnp.zeros((cap + META, LANES), jnp.bfloat16)
        return sums([none], edges, names, state, shape)

    def agreed(flag):
        return flag if bands == 2 else lax.pmax(flag, ("row", "rep"))

    (acc, cnt), edges = one_round(None, jnp.int32(0))
    flag, full_cnt, left, right = border(edges, names, (acc, cnt), shape)

    def more(carry):
        return carry[0] < carry[1][0]

    def again(carry):
        turn, _, acc, cnt, full_cnt, left, right = carry
        state, fresh = one_round((acc, cnt), turn)
        acc, cnt = late_edges(fresh, state)
        flag, full_cnt, left, right = border(edges, names, (acc, cnt), shape)
        return turn + 1, agreed(flag), acc, cnt, full_cnt, left, right

    _, _, acc, _, cnt, left, right = lax.while_loop(
        more, again, (jnp.int32(1), agreed(flag), acc, cnt, full_cnt, left, right)
    )
    peers = lax.axis_size(("col", "rep"))
    from_left = lax.ppermute(right, ("col", "rep"), [(i, i + 1) for i in range(peers - 1)])
    from_right = lax.ppermute(left, ("col", "rep"), [(i + 1, i) for i in range(peers - 1)])
    inner, edge, edge_cnt = inner_mix(edges, names, acc, cnt, left, right, codebook)
    return outer_mix(from_left, from_right, edge, edge_cnt, codebook, inner)


def solution(mesh):
    placed = (P("row", "col", "rep", None), P("row", "col", "rep"), P("row", ("col", "rep"), None))
    return jax.shard_map(
        body, mesh=mesh, in_specs=placed, out_specs=P("row", ("col", "rep"), None), check_vma=False
    )
```

```python
import functools
import math

import jax
import jax.numpy as jnp
from jax import lax
from jax.experimental import pallas as pl
from jax.experimental.pallas import tpu as pltpu
from jax.sharding import PartitionSpec as P

RADIUS = 15
LANES = 128
META = 16
HALO = 16
GROUP = 16
STATUS = 8
VMEM_LIMIT = 24 * 1024 * 1024
COST = pl.CostEstimate(flops=2**20, bytes_accessed=2**16, transcendentals=0)


def gauss(distance):
    d = distance.astype(jnp.float32)
    weight = jnp.exp(-(d * d) / (2.0 * RADIUS * RADIUS))
    return jnp.where(jnp.abs(d) <= RADIUS, weight, 0.0)


def capacity(total, share):
    mean = total * share
    spread = math.sqrt(total * share * (1.0 - share))
    return min(-(-int(mean + 4.7 * spread) // 16) * 16, -(-total // 16) * 16)


def quotient(value, by):
    if by & (by - 1) == 0:
        return lax.shift_right_logical(value, by.bit_length() - 1)
    return lax.div(value, by)


def lane_rows(total):
    return -(-total // LANES)


def side_of(side, rows):
    if side == "next":
        return jnp.int32(-rows), jnp.int32(rows - RADIUS), jnp.int32(0)
    if side == "previous":
        return jnp.int32(rows), jnp.int32(0), jnp.int32(rows - GROUP)
    top = lax.axis_index("row") == 0
    there = [jnp.where(top, a, b) for a, b in ((-rows, rows), (rows - RADIUS, 0), (rows - GROUP, 0))]
    return tuple(there)


CHUNK = 256
WINDOWS = (48, 96)


def bucket_kernel(dims, caps, side, turn_ref, x_ref, idx_ref, *rest):
    rows, block_cols, cols, reps = dims
    cap, edge_cap = caps
    owns, edges = rest[:reps], rest[reps : 2 * reps]
    wide, moved, edge_moved, onehot = rest[2 * reps :]
    me, turn = lax.axis_index("rep"), turn_ref[0]
    shift, low, _ = side_of(side, rows)
    high = low + RADIUS
    idx = idx_ref[...]
    chunks = idx.shape[0]
    r = quotient(idx, block_cols)
    c = idx - r * block_cols
    t = quotient(c, cols)
    cl = c - t * cols
    step = partner_step(me, t, reps)
    near = (r >= low) & (r < high)
    member = []
    for s in range(reps):
        here = step == s
        member += [here & near, here & jnp.logical_not(near)]
    members = jnp.concatenate([jnp.where(m, 1.0, 0.0) for m in member], axis=0)
    members16 = members.astype(jnp.bfloat16)
    count = 2 * reps * chunks
    up = lax.broadcasted_iota(jnp.int32, (LANES, LANES), 0)
    across = lax.broadcasted_iota(jnp.int32, (LANES, LANES), 1)
    tri = jnp.where(up <= across, 1.0, 0.0).astype(jnp.bfloat16)
    ones = jnp.ones((LANES, LANES), jnp.bfloat16)
    both = jnp.concatenate([tri, ones], axis=1)
    scanned = jnp.dot(members16, both, preferred_element_type=jnp.float32)
    inside, totals = scanned[:, :LANES], scanned[:, LANES:]
    i0 = lax.broadcasted_iota(jnp.int32, (count, count), 0)
    i1 = lax.broadcasted_iota(jnp.int32, (count, count), 1)
    group = 2 * chunks
    before = (quotient(i0, group) == quotient(i1, group)) & (i1 < i0)
    before = jnp.where(before, 1.0, 0.0).astype(jnp.bfloat16)
    offset = jnp.dot(before, totals.astype(jnp.bfloat16), preferred_element_type=jnp.float32)
    place = jnp.where(members > 0.5, offset + inside - 1.0, -1.0)
    ends = offset + totals
    near_count = [ends[s * group + chunks - 1 : s * group + chunks] for s in range(reps)]
    own_count = [ends[(s + 1) * group - 1 : (s + 1) * group] for s in range(reps)]
    most = functools.reduce(jnp.maximum, own_count)
    most_near = functools.reduce(jnp.maximum, near_count)
    rounds = jnp.maximum(
        jnp.floor((most + (cap - 0.5)) / cap), jnp.floor((most_near + (edge_cap - 0.5)) / edge_cap)
    )

    pad = jnp.zeros((LANES - 2 * chunks, LANES), jnp.float32)
    flat = jnp.concatenate([r.astype(jnp.float32), (cl + 1).astype(jnp.float32), pad], axis=0)
    turned = flat.T
    wide[:, :LANES] = x_ref[...]
    for k in range(chunks):
        part = turned if k == 0 else pltpu.roll(turned, LANES - k, 1)
        wide[k * LANES : (k + 1) * LANES, LANES:] = part.astype(jnp.bfloat16)

    per = CHUNK // LANES
    begin = jnp.floor(offset / 8.0) * 8.0
    line = lax.broadcasted_iota(jnp.int32, (count, LANES), 0)
    first_of_chunk = line - quotient(line, per) * per == 0
    far = (quotient(line, chunks) & 1) == 1
    room = jnp.where(far, float(WINDOWS[1]), float(WINDOWS[0]))
    reach = jnp.concatenate([ends[per - 1 :], ends[: per - 1]], axis=0) - begin
    spill = jnp.where(first_of_chunk, reach - room, 0.0)
    fits = (turn == 0) & (jnp.max(jnp.maximum(spill, most - cap)) <= 0.0)

    @pl.when(fits)
    def _():
        moved[...] = jnp.zeros_like(moved)
        starts = begin.astype(jnp.int32)
        for j in range(chunks // per):
            pieces, spots = [], []
            for s in range(reps):
                for e, window in enumerate(WINDOWS):
                    line = (2 * s + e) * chunks + j * per
                    slot = lax.broadcasted_iota(jnp.int32, (window, LANES), 0).astype(jnp.float32)
                    halves = []
                    for h in range(per):
                        target = place[line + h : line + h + 1] - begin[line : line + 1]
                        halves.append(jnp.where(slot == target, 1.0, 0.0).astype(jnp.bfloat16))
                    pieces.append(jnp.concatenate(halves, axis=1))
                    spots.append((s, window, starts[line, 0]))
            picked = jnp.dot(
                jnp.concatenate(pieces, axis=0),
                wide[j * CHUNK : (j + 1) * CHUNK, :],
                preferred_element_type=jnp.float32,
            )
            at = 0
            for s, window, spot in spots:
                span = pl.ds(pl.multiple_of(spot, 8), window)
                moved[s, span, :] = moved[s, span, :] + picked[at : at + window]
                at += window
        for s in range(reps):
            edge_moved[s] = moved[s, :edge_cap, :]

    @pl.when(jnp.logical_not(fits))
    def _():
        def gather(s, lines, size, out):
            slot = lax.broadcasted_iota(jnp.int32, (size, LANES), 0).astype(jnp.float32)
            slot = slot + (turn * size).astype(jnp.float32)
            for k in range(chunks):
                part = jnp.zeros((size, LANES), jnp.float32)
                for line in lines:
                    row = place[line * chunks + k : line * chunks + k + 1]
                    part = part + jnp.where(slot == row, 1.0, 0.0)
                onehot[:size, k * LANES : (k + 1) * LANES] = part.astype(jnp.bfloat16)
            out[s, :size, :] = jnp.dot(onehot[:size, :], wide[...], preferred_element_type=jnp.float32)

        for s in range(reps):
            gather(s, (2 * s, 2 * s + 1), cap, moved)
            gather(s, (2 * s,), edge_cap, edge_moved)

    pick_row = lax.broadcasted_iota(jnp.int32, (16, LANES), 0)
    pick_lane = lax.broadcasted_iota(jnp.int32, (16, LANES), 1)
    pick = ((pick_row == 0) & (pick_lane == 0)) | ((pick_row == 1) & (pick_lane == chunks))
    pick = jnp.where(pick, 1.0, 0.0).astype(jnp.bfloat16)
    for s in range(reps):
        for size, source, out in ((cap, moved, owns[s]), (edge_cap, edge_moved, edges[s])):
            ready = source[s, :size, :].astype(jnp.bfloat16)
            out[:size, :] = ready[:, :LANES]
            meta = lax.dot_general(
                pick, ready[:, LANES:], (((1,), (1,)), ((), ())), preferred_element_type=jnp.float32
            )
            node_row, node_col = meta[0:1], meta[1:2]
            if out is edges[s]:
                number = lax.broadcasted_iota(jnp.int32, (1, size), 1) + turn * size
                listed = number.astype(jnp.float32) < near_count[s][:, :1]
                node_col = jnp.where(listed, node_col, 0.0)
                node_row = node_row + shift.astype(jnp.float32)
            out[size:, :] = meta_rows(node_row, node_col, rounds, size).astype(jnp.bfloat16)


def meta_rows(node_row, node_col, rounds, cap):
    def split(line):
        parts = []
        for i in range(lane_rows(cap)):
            part = line[:, i * LANES : min((i + 1) * LANES, cap)]
            if part.shape[1] < LANES:
                part = jnp.concatenate([part, jnp.zeros((1, LANES - part.shape[1]), part.dtype)], axis=1)
            parts.append(part)
        return parts

    lines = split(node_col) + split(node_row) + [rounds]
    lines.append(jnp.zeros((META - len(lines), LANES), jnp.float32))
    return jnp.concatenate(lines, axis=0)


def partner_step(me, target, count):
    if count & (count - 1) == 0:
        return lax.bitwise_xor(target, jnp.full(target.shape, me, jnp.int32))
    return lax.rem(target - me + count, count)


def partner(me, step, count):
    return me ^ step if count & (count - 1) == 0 else (me + step) % count


def buckets(vec_rows, index_rows, turn, dims, caps, side):
    reps = dims[3]
    total = vec_rows.shape[0]
    deep = max(caps) + max(WINDOWS)
    messages = [jax.ShapeDtypeStruct((c + META, LANES), jnp.bfloat16) for c in caps for _ in range(reps)]
    whole = pl.BlockSpec(memory_space=pltpu.VMEM)
    out = pl.pallas_call(
        functools.partial(bucket_kernel, dims, caps, side),
        out_shape=messages,
        in_specs=[pl.BlockSpec(memory_space=pltpu.SMEM), whole, whole],
        out_specs=[whole] * (2 * reps),
        scratch_shapes=[
            pltpu.VMEM((total, 2 * LANES), jnp.bfloat16),
            pltpu.VMEM((reps, deep, 2 * LANES), jnp.float32),
            pltpu.VMEM((reps, caps[1], 2 * LANES), jnp.float32),
            pltpu.VMEM((max(caps), total), jnp.bfloat16),
        ],
        compiler_params=pltpu.CompilerParams(vmem_limit_bytes=VMEM_LIMIT),
        cost_estimate=pl.CostEstimate(
            flops=2 * reps * 1024 * total * 256, bytes_accessed=2 * total * LANES * 2, transcendentals=0
        ),
        name="buckets",
    )(turn, vec_rows, index_rows)
    return out[:reps], out[reps:]


def read_message(message, cap, shape):
    rows, cols = shape
    lines = lane_rows(cap)
    width = cap + META
    meta = message[cap:, :].astype(jnp.float32)

    def line(first):
        whole = jnp.concatenate([meta[first + j : first + j + 1] for j in range(lines)], axis=1)[:, :width]
        if whole.shape[1] < width:
            whole = jnp.concatenate([whole, jnp.zeros((1, width - whole.shape[1]), jnp.float32)], axis=1)
        return whole

    node_col, node_row = line(0), line(lines)
    here = lax.broadcasted_iota(jnp.int32, (cols, width), 0).astype(jnp.float32)
    hit = jnp.where(here == node_col - 1.0, 1.0, 0.0).astype(jnp.bfloat16)
    at = lax.broadcasted_iota(jnp.int32, (rows, width), 0).astype(jnp.float32)
    weight = gauss(at - node_row).astype(jnp.bfloat16)
    rounds = jnp.max(meta[2 * lines : 2 * lines + 1])
    return hit, weight, rounds


def weighted(picked, block, message, product):
    count, width = picked.shape
    for i in range(GROUP):
        line = jnp.broadcast_to(block[i : i + 1, :], (count, width)).astype(jnp.bfloat16)
        product[i * count : (i + 1) * count, :width] = picked * line
    total = jnp.dot(product[: GROUP * count, :width], message[...], preferred_element_type=jnp.float32)
    return total.reshape(GROUP, count, LANES)


def edge_sums(sides, names, caps, shape, pieces, weights, product, counted):
    results, rounds = [], jnp.float32(0.0)
    for n, messages in enumerate(sides):
        span = pl.ds(pl.multiple_of(side_of(names[n], shape[0])[2], GROUP), GROUP)
        total = None
        for message, cap in zip(messages, caps[n]):
            hit, weight, told = read_message(message, cap, shape)
            rounds = jnp.maximum(rounds, told)
            weights[:, : cap + META] = weight.astype(jnp.float32)
            if counted is not None:
                counted = counted + count_nodes(hit, weight)
            hits = [hit[lo:hi] for lo, hi in pieces]
            hits = hits[0] if len(hits) == 1 else jnp.concatenate(hits, axis=0)
            term = weighted(hits, weights[span, : cap + META], message, product)
            total = term if total is None else total + term
        results.append((span, total))
    return results, rounds, counted


def count_nodes(hit, weight):
    return lax.dot_general(hit, weight, (((1,), (1,)), ((), ())), preferred_element_type=jnp.float32)


def split_sides(refs, counts):
    return [[refs.pop(0) for _ in range(count)] for count in counts]


def sums_kernel(shape, caps, names, side_caps, first, *refs):
    rows, cols = shape
    refs = list(refs)
    messages = [refs.pop(0) for _ in caps]
    sides = split_sides(refs, [len(c) for c in side_caps])
    if not first:
        acc_in, cnt_in = refs.pop(0), refs.pop(0)
    acc, cnt, weights, edge_weights, product = refs
    counted = jnp.zeros((cols, rows), jnp.float32) if first else cnt_in[:cols]
    rounds = jnp.zeros((STATUS, rows), jnp.float32) if first else cnt_in[cols:]
    chosen = []
    for m, (message, cap) in enumerate(zip(messages, caps)):
        hit, weight, told = read_message(message, cap, shape)
        chosen.append(hit)
        rounds = jnp.maximum(rounds, told)
        weights[m, :, : cap + META] = weight.astype(jnp.float32)
        counted = counted + count_nodes(hit, weight)
    for start in range(0, rows, GROUP):
        span = pl.ds(start, GROUP)
        total = jnp.zeros((GROUP, cols, LANES), jnp.float32) if first else acc_in[span]
        for m, message in enumerate(messages):
            total = total + weighted(chosen[m], weights[m, span, : caps[m] + META], message, product)
        acc[span] = total
    if sides:
        totals, told, counted = edge_sums(
            sides, names, side_caps, shape, [(0, cols)], edge_weights, product, counted
        )
        rounds = jnp.maximum(rounds, told)
        for span, total in totals:
            acc[span] = acc[span] + total
    cnt[:cols] = counted
    cnt[cols:] = rounds


def sums(messages, sides, names, state, shape):
    rows, cols = shape
    caps = [m.shape[0] - META for m in messages]
    side_caps = [[m.shape[0] - META for m in side] for side in sides]
    first = state is None
    whole = pl.BlockSpec(memory_space=pltpu.VMEM)
    operands = list(messages) + [m for side in sides for m in side]
    specs = [whole] * len(operands)
    aliases = {}
    if not first:
        aliases = {len(operands): 0, len(operands) + 1: 1}
        specs += [whole, whole]
        operands += list(state)
    deep = max(caps) + META
    return pl.pallas_call(
        functools.partial(sums_kernel, shape, caps, names, side_caps, first),
        out_shape=[
            jax.ShapeDtypeStruct((rows, cols, LANES), jnp.float32),
            jax.ShapeDtypeStruct((cols + STATUS, rows), jnp.float32),
        ],
        in_specs=specs,
        out_specs=[whole, whole],
        input_output_aliases=aliases,
        scratch_shapes=[
            pltpu.VMEM((len(caps), rows, deep), jnp.float32),
            pltpu.VMEM((rows, deep), jnp.float32),
            pltpu.VMEM((GROUP * cols, deep), jnp.bfloat16),
        ],
        compiler_params=pltpu.CompilerParams(vmem_limit_bytes=VMEM_LIMIT),
        cost_estimate=COST,
        name="sums",
    )(*operands)


def border_kernel(shape, names, side_caps, *refs):
    rows, cols = shape
    refs = list(refs)
    sides = split_sides(refs, [len(c) for c in side_caps])
    acc, cnt_in, flag, cnt, left, right, weights, product = refs
    left[:rows] = acc[:, :HALO, :].astype(jnp.bfloat16)
    right[:rows] = acc[:, cols - HALO :, :].astype(jnp.bfloat16)
    totals, told, counted = edge_sums(
        sides, names, side_caps, shape, [(0, HALO), (cols - HALO, cols)], weights, product, cnt_in[:cols]
    )
    for span, total in totals:
        left[span] = (total[:, :HALO] + acc[span, :HALO, :]).astype(jnp.bfloat16)
        right[span] = (total[:, HALO:] + acc[span, cols - HALO :, :]).astype(jnp.bfloat16)
    cnt[...] = counted
    flag[0] = jnp.max(jnp.maximum(told, cnt_in[cols:])).astype(jnp.int32)
    fill = [jnp.zeros((cols, LANES - rows), jnp.float32)] if rows < LANES else []
    lane_counts = jnp.concatenate([counted] + fill, axis=1).astype(jnp.bfloat16)
    left[rows : rows + 1] = lane_counts[:HALO][None]
    right[rows : rows + 1] = lane_counts[cols - HALO :][None]


def border(sides, names, state, shape):
    rows, cols = shape
    smem = pl.BlockSpec(memory_space=pltpu.SMEM)
    whole = pl.BlockSpec(memory_space=pltpu.VMEM)
    halo = jax.ShapeDtypeStruct((rows + 1, HALO, LANES), jnp.bfloat16)
    edges = [m for side in sides for m in side]
    side_caps = [[m.shape[0] - META for m in side] for side in sides]
    deep = edges[0].shape[0]
    return pl.pallas_call(
        functools.partial(border_kernel, shape, names, side_caps),
        out_shape=[
            jax.ShapeDtypeStruct((1,), jnp.int32),
            jax.ShapeDtypeStruct((cols, rows), jnp.float32),
            halo,
            halo,
        ],
        in_specs=[whole] * (len(edges) + 2),
        out_specs=[smem, whole, whole, whole],
        scratch_shapes=[
            pltpu.VMEM((rows, deep), jnp.float32),
            pltpu.VMEM((GROUP * 2 * HALO, deep), jnp.bfloat16),
        ],
        compiler_params=pltpu.CompilerParams(vmem_limit_bytes=VMEM_LIMIT),
        cost_estimate=COST,
        name="border",
    )(*edges, *state)


def band_matrix(outs, ins, first_out, first_in, repeat):
    down = lax.broadcasted_iota(jnp.int32, (repeat * outs, repeat * ins), 0)
    across = lax.broadcasted_iota(jnp.int32, (repeat * outs, repeat * ins), 1)
    top, side = quotient(down, outs), quotient(across, ins)
    away = (across - side * ins + first_in) - (down - top * outs + first_out)
    return jnp.where(top == side, gauss(away), 0.0).astype(jnp.bfloat16)


def inner_kernel(shape, names, side_caps, *refs):
    rows, cols = shape
    refs = list(refs)
    sides = split_sides(refs, [len(c) for c in side_caps])
    acc, cnt, left, right, codebook, out, edge, edge_cnt, weights, product, ready, own, sem = refs
    middle = slice(HALO, cols - HALO)
    own[:, middle, :] = acc[:, middle, :].astype(jnp.bfloat16)
    own[:, :HALO, :] = left[:rows]
    own[:, cols - HALO :, :] = right[:rows]
    totals, _, _ = edge_sums(sides, names, side_caps, shape, [(HALO, cols - HALO)], weights, product, None)
    for span, total in totals:
        own[span, middle, :] = (total + acc[span, middle, :]).astype(jnp.bfloat16)
    band = band_matrix(cols, cols, 0, 0, 1)
    counted = jnp.dot(band, cnt[...].astype(jnp.bfloat16), preferred_element_type=jnp.float32)
    edge_cnt[:HALO] = counted[:HALO]
    edge_cnt[HALO:] = counted[cols - HALO :]
    scale = 0.7 / (counted[HALO : cols - HALO] + 1.0)
    pair = band_matrix(cols, cols, 0, 0, 2)
    copies = []
    for start in range(0, rows, GROUP):
        span = pl.ds(start, GROUP)
        for i in range(start, start + GROUP, 4):
            twos = [jnp.concatenate([own[i + 2 * j], own[i + 2 * j + 1]], axis=0) for j in range(2)]
            smooth = jnp.dot(pair, jnp.concatenate(twos, axis=1), preferred_element_type=jnp.float32)
            for j in range(4):
                a = i + j
                mine = smooth[(j % 2) * cols : (j % 2 + 1) * cols, (j // 2) * LANES : (j // 2 + 1) * LANES]
                edge[a, :HALO, :] = mine[:HALO]
                edge[a, HALO:, :] = mine[cols - HALO :]
                old = codebook[a, HALO : cols - HALO, :].astype(jnp.float32)
                fresh = 0.3 * old + mine[HALO : cols - HALO] * scale[:, a : a + 1]
                ready[a] = fresh.astype(jnp.bfloat16)
        copies.append(
            pltpu.make_async_copy(ready.at[span], out.at[span, HALO : cols - HALO, :], sem.at[start // GROUP])
        )
        copies[-1].start()
    for copy in copies:
        copy.wait()


def outer_kernel(shape, side, halo, edge, edge_cnt, codebook, inner, out, ready, sem):
    rows, cols = shape
    del inner
    eight = LANES // HALO
    copies = []
    first_out, first_in = ((0, -HALO), (cols - HALO, cols))[side]
    columns = slice(first_out, first_out + HALO)
    band = band_matrix(HALO, HALO, first_out, first_in, 1)
    counted = jnp.dot(band, halo[rows], preferred_element_type=jnp.float32)[:, :rows]
    counted = counted + edge_cnt[side * HALO : (side + 1) * HALO]
    scale = 0.7 / (counted + 1.0)
    blocks = band_matrix(HALO, HALO, first_out, first_in, eight)
    for step, start in enumerate(range(0, rows, 2 * eight)):
        there = [halo[start + j * eight : start + (j + 1) * eight].reshape(LANES, LANES) for j in range(2)]
        smooth = jnp.dot(blocks, jnp.concatenate(there, axis=1), preferred_element_type=jnp.float32)
        for j in range(2 * eight):
            a = start + j
            top, lane = (j % eight) * HALO, (j // eight) * LANES
            mine = smooth[top : top + HALO, lane : lane + LANES]
            mine = mine + edge[a, side * HALO : (side + 1) * HALO, :]
            fresh = 0.3 * codebook[a, columns, :].astype(jnp.float32) + mine * scale[:, a : a + 1]
            ready[a] = fresh.astype(jnp.bfloat16)
        span = pl.ds(start, 2 * eight)
        copies.append(pltpu.make_async_copy(ready.at[span], out.at[span, columns, :], sem.at[step]))
        copies[-1].start()
    for copy in copies:
        copy.wait()


def inner_mix(sides, names, acc, cnt, left, right, codebook):
    rows, cols, width = codebook.shape
    whole = pl.BlockSpec(memory_space=pltpu.VMEM)
    edges = [m for side in sides for m in side]
    side_caps = [[m.shape[0] - META for m in side] for side in sides]
    deep = edges[0].shape[0]
    middle = cols - 2 * HALO
    return pl.pallas_call(
        functools.partial(inner_kernel, (rows, cols), names, side_caps),
        out_shape=[
            jax.ShapeDtypeStruct(codebook.shape, jnp.bfloat16),
            jax.ShapeDtypeStruct((rows, 2 * HALO, width), jnp.float32),
            jax.ShapeDtypeStruct((2 * HALO, rows), jnp.float32),
        ],
        in_specs=[whole] * (len(edges) + 5),
        out_specs=[pl.BlockSpec(memory_space=pl.ANY), whole, whole],
        scratch_shapes=[
            pltpu.VMEM((rows, deep), jnp.float32),
            pltpu.VMEM((GROUP * middle, deep), jnp.bfloat16),
            pltpu.VMEM((rows, middle, width), jnp.bfloat16),
            pltpu.VMEM((rows, cols, width), jnp.bfloat16),
            pltpu.SemaphoreType.DMA((rows // GROUP,)),
        ],
        compiler_params=pltpu.CompilerParams(vmem_limit_bytes=VMEM_LIMIT),
        cost_estimate=COST,
        name="inner",
    )(*edges, acc, cnt, left, right, codebook)


def outer_mix(side, halo, edge, edge_cnt, codebook, inner):
    rows, cols, width = codebook.shape
    whole = pl.BlockSpec(memory_space=pltpu.VMEM)
    anywhere = pl.BlockSpec(memory_space=pl.ANY)
    return pl.pallas_call(
        functools.partial(outer_kernel, (rows, cols), side),
        out_shape=jax.ShapeDtypeStruct(codebook.shape, jnp.bfloat16),
        in_specs=[whole] * 4 + [anywhere],
        out_specs=anywhere,
        input_output_aliases={4: 0},
        scratch_shapes=[
            pltpu.VMEM((rows, HALO, width), jnp.bfloat16),
            pltpu.SemaphoreType.DMA((rows * HALO // (2 * LANES),)),
        ],
        compiler_params=pltpu.CompilerParams(vmem_limit_bytes=VMEM_LIMIT),
        name="outer",
    )(halo, edge, edge_cnt, codebook, inner)


def body(vectors, best_node, codebook):
    rows, cols, width = codebook.shape
    reps, bands = lax.axis_size("rep"), lax.axis_size("row")
    dims = (rows, cols * reps, cols, reps)
    shape = (rows, cols)
    vec_rows = vectors.reshape(-1, width)
    total = vec_rows.shape[0]
    index_rows = best_node.reshape(-1, LANES)
    cap = capacity(total, 1.0 / reps)
    edge_cap = capacity(total, RADIUS / rows / reps)

    if bands == 2:
        sides = {"other": [(0, 1), (1, 0)]}
    else:
        sides = {
            "next": [(i, i + 1) for i in range(bands - 1)],
            "previous": [(i + 1, i) for i in range(bands - 1)],
        }
    names = list(sides)

    def send_own(own):
        return [
            lax.ppermute(own[s], "rep", [(i, partner(i, s, reps)) for i in range(reps)])
            for s in range(1, reps)
        ]

    def send_edges(near, pairs, ahead):
        arrived = []
        for s, message in enumerate(near):
            if s >= ahead:
                message, arrived[s - ahead] = lax.optimization_barrier((message, arrived[s - ahead]))
            joint = [(a * reps + i, b * reps + partner(i, s, reps)) for a, b in pairs for i in range(reps)]
            arrived.append(lax.ppermute(message, ("row", "rep"), joint))
        return arrived

    def one_round(state, turn):
        near = []
        for name in names:
            own, edge = buckets(vec_rows, index_rows, jnp.reshape(turn, (1,)), dims, (cap, edge_cap), name)
            mine = mine if near else own
            near.append(edge)
        arrived = send_own(mine)
        state = sums([mine[0]], [], names, state, shape)
        near, state = lax.optimization_barrier((near, state))
        edges = [send_edges(edge, sides[name], 2) for edge, name in zip(near, names)]
        for message in arrived:
            state = sums([message], [], names, state, shape)
        return state, edges

    def late_edges(edges, state):
        none = jnp.zeros((cap + META, LANES), jnp.bfloat16)
        return sums([none], edges, names, state, shape)

    def agreed(flag):
        return flag if bands == 2 else lax.pmax(flag, ("row", "rep"))

    (acc, cnt), edges = one_round(None, jnp.int32(0))
    flag, full_cnt, left, right = border(edges, names, (acc, cnt), shape)

    def more(carry):
        return carry[0] < carry[1][0]

    def again(carry):
        turn, _, acc, cnt, full_cnt, left, right = carry
        state, fresh = one_round((acc, cnt), turn)
        acc, cnt = late_edges(fresh, state)
        flag, full_cnt, left, right = border(edges, names, (acc, cnt), shape)
        return turn + 1, agreed(flag), acc, cnt, full_cnt, left, right

    _, _, acc, _, cnt, left, right = lax.while_loop(
        more, again, (jnp.int32(1), agreed(flag), acc, cnt, full_cnt, left, right)
    )
    peers = lax.axis_size(("col", "rep"))
    from_left = lax.ppermute(right, ("col", "rep"), [(i, i + 1) for i in range(peers - 1)])
    from_right = lax.ppermute(left, ("col", "rep"), [(i + 1, i) for i in range(peers - 1)])
    inner, edge, edge_cnt = inner_mix(edges, names, acc, cnt, left, right, codebook)
    half = outer_mix(1, from_right, edge, edge_cnt, codebook, inner)
    return outer_mix(0, from_left, edge, edge_cnt, codebook, half)


def solution(mesh):
    placed = (P("row", "col", "rep", None), P("row", "col", "rep"), P("row", ("col", "rep"), None))
    return jax.shard_map(
        body, mesh=mesh, in_specs=placed, out_specs=P("row", ("col", "rep"), None), check_vma=False
    )
```
